32 devices in a mesh: grid: 8 (over z, y), space: 4 (over x, core).
Axes of the slice: x: 2, y: 2, z: 4, core: 2. Of those that a mesh axis runs over, the one named last changes fastest.
Arguments:
- density: float32 [8, 512, 64, 128], P('grid', 'space'), may hold values from -6 to 6
- kappa: float32 [8, 512, 64, 128], P('grid', 'space'), may hold values from 0.02 to 0.16
- levels: int32 [8, 3], P('grid'), may hold values from 3 to 6, as said below
- coefs: int32 [8], P('grid'), may hold values from -2 to 1, as said below
Outputs:
- combined: float32 [8, 512, 64, 128], P('grid', 'space')
The draws below stay inside these ranges and needn't reach their ends.
Inputs may be any that keep to these rules, and one draw needn't show every extreme that they name: `levels`: each level vector is (3, 3, 3) plus nonnegative integers summing to 1, 2 or 3, no two grids alike; a level at or above log2 of an axis's cells keeps that whole axis. coefs[g] is +1 where the grid's levels sum to 12 or 10 and -2 where they sum to 11.
All inputs are finite; a program needn't handle non-finite values.
Results may differ from the reference program's by a relative error of at most 0.0003.
Values sent between devices are 32-bit elements; how exact they have to be, the bound alone decides.
A program may use at most 128 MiB of HBM per device.

```python
import math
import jax
import jax.numpy as jnp
import numpy as np
from jax import lax

X = 512
Y = 64
Z = 128
ITERS = 8
GRIDS = 8


def ordered_offsets(key):
    extremes = [(3, 0, 0), (0, 3, 0), (0, 0, 3)]
    middle = []
    others = []
    for first in range(4):
        for second in range(4):
            for third in range(4):
                total_k = first + second + third
                vector = (first, second, third)
                if vector in extremes:
                    continue
                if total_k == 2:
                    middle.append(vector)
                elif total_k == 1 or total_k == 3:
                    others.append(vector)
    middle_table = jnp.asarray(np.array(middle, dtype=np.int32))
    other_table = jnp.asarray(np.array(others, dtype=np.int32))
    extreme_table = jnp.asarray(np.array(extremes, dtype=np.int32))
    key_middle = jax.random.fold_in(key, 11)
    key_rest = jax.random.fold_in(key, 12)
    middle_order = jax.random.permutation(key_middle, middle_table.shape[0])
    shuffled_middle = jnp.take(middle_table, middle_order, axis=0)
    rest = jnp.concatenate([shuffled_middle[1:], other_table], axis=0)
    rest_order = jax.random.permutation(key_rest, rest.shape[0])
    rest = jnp.take(rest, rest_order, axis=0)
    return jnp.concatenate([extreme_table, shuffled_middle[0:1], rest], axis=0)


def draw_levels(key, part):
    offsets = ordered_offsets(key)
    return (offsets[:GRIDS] + 3).astype(jnp.int32)


def draw_coefs(key, part):
    offsets = ordered_offsets(key)[:GRIDS]
    summed = jnp.sum(offsets, axis=1)
    return jnp.where(summed == 2, -2, 1).astype(jnp.int32)


def block_levels(stream_key, shape, pieces, least, high):
    factor_of, own = 1.0, jax.random.fold_in(stream_key, 6)
    for position, parts in pieces:
        heights = jnp.exp(jax.random.uniform(jax.random.fold_in(own, position), (parts,), jnp.float32, least / len(pieces), high / len(pieces)))
        factor_of = factor_of * jnp.repeat(heights, shape[position] // parts).reshape([-1 if axis == position else 1 for axis in range(len(shape))])
    return factor_of


def bell_draw(key, extent, spread, bound, cuts=(), kind=jnp.bfloat16):
    values = spread * jax.random.normal(key, extent, jnp.float32)
    if cuts:
        values = values * block_levels(key, extent, cuts, -0.22, 0.18)
    return jnp.clip(values, -bound, bound).astype(kind)


def setup_inputs(seed: int = 0) -> dict:
    splits = jax.random.split(jax.random.key(seed), 5)
    return {
        "density": bell_draw(splits[0], (GRIDS, X, Y, Z), 1.0, 6.0, ((0, 8), (1, 4)), jnp.float32),
        "kappa": jnp.clip(jnp.exp(math.log(0.16) - 2.0794415 * jax.random.uniform(splits[1], (GRIDS, X, Y, Z), jnp.float32) ** block_levels(splits[1], (GRIDS, X, Y, Z), ((0, 8), (1, 4)), -0.2, 0.2)), 0.02, 0.16),
        "levels": draw_levels(jax.random.fold_in(splits[4], 71), 0),
        "coefs": draw_coefs(jax.random.fold_in(splits[4], 71), 0),
    }


def build_tables(count):
    depth = count.bit_length() - 1
    hier = np.eye(count)
    dehier = np.eye(count)
    level_table = np.zeros(count, dtype=np.int64)
    for index in range(1, count):
        trailing = 0
        while (index >> trailing) & 1 == 0:
            trailing += 1
        spacing = 1 << trailing
        level_table[index] = depth - trailing
        hier[index, (index - spacing) % count] -= 0.5
        hier[index, (index + spacing) % count] -= 0.5
    for trailing in range(depth - 1, -1, -1):
        spacing = 1 << trailing
        for index in range(spacing, count, 2 * spacing):
            dehier[index] = dehier[index] + 0.5 * (dehier[(index - spacing) % count] + dehier[(index + spacing) % count])
    return jnp.asarray(hier, jnp.float32), jnp.asarray(dehier, jnp.float32), jnp.asarray(level_table.astype(np.int32))


def transform_all(field, mat_x, mat_y, mat_z):
    hi = lax.Precision.HIGHEST
    field = jnp.einsum("wx,gxyz->gwyz", mat_x, field, precision=hi)
    field = jnp.einsum("vy,gxyz->gxvz", mat_y, field, precision=hi)
    return jnp.einsum("gxyz,wz->gxyw", field, mat_z, precision=hi)


def reference(density, kappa, levels, coefs):
    hier_x, dehier_x, level_x = build_tables(X)
    hier_y, dehier_y, level_y = build_tables(Y)
    hier_z, dehier_z, level_z = build_tables(Z)
    faces = []
    for axis in (1, 2, 3):
        faces.append(0.5 * (kappa + jnp.roll(kappa, -1, axis)))
        faces.append(0.5 * (kappa + jnp.roll(kappa, 1, axis)))
    field = density
    for sweep_index in range(ITERS):
        flux = faces[0] * (jnp.roll(field, -1, 1) - field) + faces[1] * (jnp.roll(field, 1, 1) - field)
        flux = flux + faces[2] * (jnp.roll(field, -1, 2) - field) + faces[3] * (jnp.roll(field, 1, 2) - field)
        flux = flux + faces[4] * (jnp.roll(field, -1, 3) - field) + faces[5] * (jnp.roll(field, 1, 3) - field)
        field = field + flux
    surplus = transform_all(field, hier_x, hier_y, hier_z)
    mask_x = (level_x[None, :] <= levels[:, 0:1]).astype(jnp.float32)
    mask_y = (level_y[None, :] <= levels[:, 1:2]).astype(jnp.float32)
    mask_z = (level_z[None, :] <= levels[:, 2:3]).astype(jnp.float32)
    mask = mask_x[:, :, None, None] * mask_y[:, None, :, None] * mask_z[:, None, None, :]
    weight = coefs.astype(jnp.float32)[:, None, None, None]
    total = jnp.sum(weight * mask * surplus, axis=0)
    return transform_all(mask * total[None], dehier_x, dehier_y, dehier_z)
```

```python
import functools

import jax
import jax.numpy as jnp
import numpy as np
from jax import lax
from jax.experimental import pallas as pl
from jax.experimental.pallas import tpu as pltpu
from jax.sharding import PartitionSpec as P

ITERS = 8
BASE = 3
EXTRA = 3
TOP = BASE + EXTRA
LANES = 128
VMEM_LIMIT = 56 * 1024 * 1024


def trailing_zeros(index):
    return (index & -index).bit_length() - 1


def level_of(index, count):
    return 0 if index == 0 else count.bit_length() - 1 - trailing_zeros(index)


def excess_of(index, count):
    return max(level_of(index, count) - BASE, 0)


def kept_indices(count):
    kept = [i for i in range(count) if level_of(i, count) <= TOP]
    return sorted(kept, key=lambda i: (excess_of(i, count), i))


def matrices(count):
    depth = count.bit_length() - 1
    hier = np.eye(count)
    dehier = np.eye(count)
    for index in range(1, count):
        spacing = 1 << trailing_zeros(index)
        hier[index, (index - spacing) % count] -= 0.5
        hier[index, (index + spacing) % count] -= 0.5
    for trailing in range(depth - 1, -1, -1):
        spacing = 1 << trailing
        for index in range(spacing, count, 2 * spacing):
            dehier[index] += 0.5 * (dehier[(index - spacing) % count] + dehier[(index + spacing) % count])
    return hier, dehier


def axis_tables(width_y, width_z):
    hier_y, dehier_y = matrices(width_y)
    hier_z, dehier_z = matrices(width_z)
    kept_y, kept_z = kept_indices(width_y), kept_indices(width_z)
    groups = width_y // 8
    order = [s * groups + j for j in range(groups) for s in range(8)]
    hy = hier_y[kept_y][:, order]
    dy = dehier_y[:, kept_y]
    hz = np.zeros((width_z, LANES))
    hz[:, : len(kept_z)] = hier_z[kept_z].T
    dz = np.zeros((LANES, width_z))
    dz[: len(kept_z)] = dehier_z[:, kept_z].T
    level_y = np.array([level_of(i, width_y) for i in kept_y])
    level_z = np.full(LANES, 99)
    level_z[: len(kept_z)] = [level_of(i, width_z) for i in kept_z]
    shape = (len(kept_y), LANES)
    ly = np.broadcast_to(level_y[:, None], shape).astype(np.int32)
    lz = np.broadcast_to(level_z[None, :], shape).astype(np.int32)
    as_bf16 = lambda m: jnp.asarray(m, jnp.bfloat16)
    return as_bf16(hy), as_bf16(hz), as_bf16(dy), as_bf16(dz), jnp.asarray(ly), jnp.asarray(lz)


class Plan:
    def __init__(self, members, slab, width_y, width_z):
        width_x = members * slab
        self.members = members
        self.stride = max(1, width_x >> TOP)
        self.rows = slab // self.stride
        kept_y = kept_indices(width_y)
        kept_z = kept_indices(width_z)
        self.blocks = len(kept_y) // 8
        block_excess = [max(excess_of(i, width_y) for i in kept_y[8 * q : 8 * q + 8]) for q in range(self.blocks)]
        width_of = [sum(excess_of(i, width_z) <= e for i in kept_z) for e in range(EXTRA + 1)]
        indices = [p * slab for p in range(members)] + [k * self.stride for k in range(1, self.rows)]
        self.levels = [level_of(i, width_x) for i in indices]
        pieces = []
        for row, index in enumerate(indices):
            for q in range(self.blocks):
                left = EXTRA - excess_of(index, width_x) - block_excess[q]
                if left >= 0:
                    pieces.append((width_of[left], row, q))
        pieces.sort(key=lambda piece: (-piece[0], piece[1], piece[2]))
        self.pieces, at = [], 0
        for width, row, q in pieces:
            if at % LANES + width > LANES:
                at += LANES - at % LANES
            self.pieces.append((row, q, at // LANES, at % LANES))
            at += width
        self.tiles = -(-at // LANES)


def split_dot(left, right, exact_left):
    value = right if exact_left else left
    high = value.astype(jnp.bfloat16)
    low = (value - high.astype(jnp.float32)).astype(jnp.bfloat16)
    dot = functools.partial(jnp.dot, preferred_element_type=jnp.float32)
    if exact_left:
        return dot(left, high) + dot(left, low)
    return dot(high, right) + dot(low, right)


def next_lane(v):
    return pltpu.roll(v, LANES - 1, 1)


def last_lane(v):
    return pltpu.roll(v, 1, 1)


def row_update(f, above, flux_below, fx, fy, fz, groups):
    gx = [fx[j] * (above[j] - f[j]) for j in range(groups)]
    follow = f[1:] + [pltpu.roll(f[0], 7, 0)]
    gy = [fy[j] * (follow[j] - f[j]) for j in range(groups)]
    before = [pltpu.roll(gy[-1], 1, 0)] + gy[:-1]
    new = []
    for j in range(groups):
        gz = fz[j] * (next_lane(f[j]) - f[j])
        plus = (f[j] + gx[j]) + (gy[j] + gz)
        minus = (flux_below[j] + before[j]) + last_lane(gz)
        new.append(plus - minus)
    return new, gx


def diffuse_kernel(plan, slab, groups, chunk, dens, kap, dprev, kprev, dnext, knext, hy, hz, out, raw_d, raw_k, f, fx, fy, fz, sems):
    halo = ITERS
    chunks = slab // chunk
    copies = []
    for c in range(chunks):
        part = pl.ds(c * chunk, chunk)
        pair = (
            pltpu.make_async_copy(kap.at[0, part], raw_k.at[part], sems.at[0, c]),
            pltpu.make_async_copy(dens.at[0, part], raw_d.at[part], sems.at[1, c]),
        )
        for copy in pair:
            copy.start()
        copies.append(pair)

    def natural(ref, row):
        return [ref[row, pl.ds(j, 8, stride=groups), :] for j in range(groups)]

    def stored(ref, row):
        return [ref[row, j] for j in range(groups)]

    def put(ref, row, values):
        for j in range(groups):
            ref[row, j] = values[j]

    def first(r, k_above, d_above, carry):
        k, d, flux = carry
        x_face = [0.5 * (k[j] + k_above[j]) for j in range(groups)]
        k_next = k[1:] + [pltpu.roll(k[0], 7, 0)]
        y_face = [0.5 * (k[j] + k_next[j]) for j in range(groups)]
        z_face = [0.5 * (k[j] + next_lane(k[j])) for j in range(groups)]
        put(fx, r - 1, x_face)
        put(fy, r - 1, y_face)
        put(fz, r - 1, z_face)
        new, flux = row_update(d, d_above, flux, x_face, y_face, z_face, groups)
        put(f, r - 1, new)
        return k_above, d_above, flux

    zero = [jnp.zeros((8, LANES), jnp.float32)] * groups
    carry = (natural(kprev, 0), natural(dprev, 0), zero)
    carry = lax.fori_loop(1, halo, lambda r, c: first(r, natural(kprev, r), natural(dprev, r), c), carry)
    for c in range(chunks):
        for copy in copies[c]:
            copy.wait()
        carry = lax.fori_loop(
            halo + c * chunk,
            halo + (c + 1) * chunk,
            lambda r, v: first(r, natural(raw_k, r - halo), natural(raw_d, r - halo), v),
            carry,
        )
    first(slab + halo, natural(knext, 0), natural(dnext, 0), carry)

    stride = plan.stride
    left = ITERS - 2
    while 2 * left + 1 >= stride:
        low, high = halo - left, halo + slab - stride + left
        low -= (high - low + 1) % 2

        def pair_step(i, carry, low=low):
            row, flux = carry
            for u in range(2):
                r = low + 2 * i + u
                above = stored(f, r + 1)
                new, flux = row_update(row, above, flux, stored(fx, r), stored(fy, r), stored(fz, r), groups)
                put(f, r, new)
                row = above
            return row, flux

        row = stored(f, low)
        below = stored(f, low - 1)
        face = stored(fx, low - 1)
        flux = [face[j] * (row[j] - below[j]) for j in range(groups)]
        lax.fori_loop(0, (high - low + 1) // 2, pair_step, (row, flux))
        left -= 1

    def cone(center, wanted, left):
        def near(j, reach):
            return any(min((j - w) % groups, (w - j) % groups) <= reach for w in wanted)

        for reach in range(left, -1, -1):
            flux = {}
            for offset in range(-reach, reach + 1):
                need = [j for j in range(groups) if near(j, reach - abs(offset))]
                r = center + offset
                cells = {}

                def cell(j):
                    if j not in cells:
                        cells[j] = f[r, j]
                    return cells[j]

                below, flux, fluxes_y, results = flux, {}, {}, {}

                def flux_y(j):
                    if j not in fluxes_y:
                        follow = cell(j + 1) if j + 1 < groups else pltpu.roll(cell(0), 7, 0)
                        fluxes_y[j] = fy[r, j] * (follow - cell(j))
                    return fluxes_y[j]

                for j in need:
                    here = cell(j)
                    flux[j] = fx[r, j] * (f[r + 1, j] - here)
                    lower = below[j] if j in below else fx[r - 1, j] * (here - f[r - 1, j])
                    before = flux_y(j - 1) if j else pltpu.roll(flux_y(groups - 1), 1, 0)
                    gz = fz[r, j] * (next_lane(here) - here)
                    results[j] = ((here + flux[j]) + (flux_y(j) + gz)) - ((lower + before) + last_lane(gz))
                for j in need:
                    f[r, j] = results[j]

    period = min(4, plan.rows)

    def cones(i, _):
        for k in range(period):
            spare = EXTRA - (0 if k == 0 else max(0, EXTRA - trailing_zeros(k)))
            if k == 0 and period < 4:
                spare = EXTRA
            step = max(1, groups >> spare)
            cone(halo + (i * period + k) * stride, list(range(0, groups, step)), left)
        return 0

    lax.fori_loop(0, plan.rows // period, cones, 0)

    for k in range(plan.rows):
        plane = f[halo + k * stride].reshape(groups * 8, LANES)
        out[k] = split_dot(split_dot(hy[...], plane, True), hz[...], False)


def grid_mask(levels, ly, lz):
    return (ly[...] <= levels[0, 1]) & (lz[...] <= levels[0, 2])


def pack_kernel(plan, pos_ref, levels, coefs, ly, lz, planes, coarse, out):
    mask = grid_mask(levels, ly, lz)
    weight = coefs[0].astype(jnp.float32)
    members, rows = plan.members, plan.rows
    surplus = []
    for p in range(members):
        if p == 0:
            value = coarse[0]
        else:
            h = 1 << trailing_zeros(p)
            value = coarse[p] - 0.5 * (coarse[p - h] + coarse[(p + h) % members])
        surplus.append(value)
    following = coarse[lax.rem(pos_ref[0] + 1, members)]
    for k in range(1, rows):
        h = 1 << trailing_zeros(k)
        above = planes[k + h] if k + h < rows else following
        surplus.append(planes[k] - 0.5 * (planes[k - h] + above))
    for row in range(len(surplus)):
        scale = jnp.where(plan.levels[row] <= levels[0, 0], weight, 0.0)
        surplus[row] = jnp.where(mask, scale * surplus[row], 0.0)
    tiles = [None] * plan.tiles
    for row, q, tile, lane in plan.pieces:
        piece = surplus[row][8 * q : 8 * q + 8]
        if lane:
            piece = pltpu.roll(piece, lane, 1)
        tiles[tile] = piece if tiles[tile] is None else tiles[tile] + piece
    for tile in range(plan.tiles):
        out[tile] = tiles[tile]


def expand_kernel(plan, slab, pos_ref, levels, ly, lz, dy, dz, packed, out, coarse, nodes, buf, sems):
    mask = grid_mask(levels, ly, lz)
    members, rows, stride = plan.members, plan.rows, plan.stride
    where = {(row, q): (tile, lane) for row, q, tile, lane in plan.pieces}

    def total(row):
        parts = []
        for q in range(plan.blocks):
            if (row, q) in where:
                tile, lane = where[row, q]
                piece = packed[tile]
                if lane:
                    piece = pltpu.roll(piece, LANES - lane, 1)
                keep = mask[8 * q : 8 * q + 8] & (plan.levels[row] <= levels[0, 0])
                parts.append(jnp.where(keep, piece, 0.0))
            else:
                parts.append(jnp.zeros((8, LANES), jnp.float32))
        return jnp.concatenate(parts, axis=0)

    values = [total(p) for p in range(members)]
    h = members // 2
    while h:
        for p in range(h, members, 2 * h):
            values[p] = values[p] + 0.5 * (values[p - h] + values[(p + h) % members])
        h //= 2
    for p in range(members):
        coarse[p] = values[p]
    pos = pos_ref[0]
    fine = [coarse[pos]] + [total(members + k - 1) for k in range(1, rows)] + [coarse[lax.rem(pos + 1, members)]]
    h = rows // 2
    while h:
        for k in range(h, rows, 2 * h):
            fine[k] = fine[k] + 0.5 * (fine[k - h] + fine[k + h])
        h //= 2
    for k in range(rows + 1):
        nodes[k] = split_dot(dy[...], split_dot(fine[k], dz[...], False), True)

    def chunk(k):
        part = pl.ds(k * stride, stride)
        return pltpu.make_async_copy(buf.at[part], out.at[0, part], sems.at[k])

    def fill(k, _):
        here = nodes[k]
        step = (nodes[k + 1] - here) * (1.0 / stride)
        for j in range(stride):
            buf[k * stride + j] = here + float(j) * step if j else here
        chunk(k).start()
        return 0

    lax.fori_loop(0, rows, fill, 0)

    def drain(k, _):
        chunk(k).wait()
        return 0

    lax.fori_loop(0, rows, drain, 0)


def local(plan, density, kappa, levels, coefs):
    _, slab, width_y, width_z = density.shape
    groups = width_y // 8
    members = lax.axis_size("space")
    position = lax.axis_index("space")
    hy, hz, dy, dz, ly, lz = axis_tables(width_y, width_z)
    pos = jnp.reshape(position, (1,)).astype(jnp.int32)
    up = [(i, (i + 1) % members) for i in range(members)]
    down = [(j, i) for i, j in up]
    dprev = lax.ppermute(density[0, slab - ITERS :], "space", up)
    kprev = lax.ppermute(kappa[0, slab - ITERS :], "space", up)
    dnext = lax.ppermute(density[0, :1], "space", down)
    knext = lax.ppermute(kappa[0, :1], "space", down)

    vmem = pl.BlockSpec(memory_space=pltpu.VMEM)
    smem = pl.BlockSpec(memory_space=pltpu.SMEM)
    anywhere = pl.BlockSpec(memory_space=pl.ANY)
    params = pltpu.CompilerParams(vmem_limit_bytes=VMEM_LIMIT)
    kept = ly.shape[0]
    chunk = min(32, slab)
    extended = pltpu.VMEM((slab + ITERS, groups, 8, LANES), jnp.float32)
    raw = pltpu.VMEM((slab, width_y, width_z), jnp.float32)
    planes = pl.pallas_call(
        functools.partial(diffuse_kernel, plan, slab, groups, chunk),
        out_shape=jax.ShapeDtypeStruct((plan.rows, kept, LANES), jnp.float32),
        in_specs=[anywhere, anywhere] + [vmem] * 6,
        out_specs=vmem,
        scratch_shapes=[raw, raw, extended, extended, extended, extended, pltpu.SemaphoreType.DMA((2, slab // chunk))],
        compiler_params=params,
        name="diffuse",
    )(density, kappa, dprev, kprev, dnext, knext, hy, hz)

    coarse = lax.all_gather(planes[0], "space", axis=0)
    packed = pl.pallas_call(
        functools.partial(pack_kernel, plan),
        out_shape=jax.ShapeDtypeStruct((plan.tiles, 8, LANES), jnp.float32),
        in_specs=[smem, smem, smem] + [vmem] * 4,
        out_specs=vmem,
        compiler_params=params,
        name="pack",
    )(pos, levels, coefs, ly, lz, planes, coarse)

    packed = lax.psum(packed, "grid")

    return pl.pallas_call(
        functools.partial(expand_kernel, plan, slab),
        out_shape=jax.ShapeDtypeStruct(density.shape, jnp.float32),
        in_specs=[smem, smem] + [vmem] * 5,
        out_specs=anywhere,
        scratch_shapes=[
            pltpu.VMEM((plan.members, kept, LANES), jnp.float32),
            pltpu.VMEM((plan.rows + 1, width_y, width_z), jnp.float32),
            raw,
            pltpu.SemaphoreType.DMA((plan.rows,)),
        ],
        compiler_params=params,
        name="expand",
    )(pos, levels, ly, lz, dy, dz, packed)


def solution(mesh):
    def whole(density, kappa, levels, coefs):
        members = mesh.shape["space"]
        plan = Plan(members, density.shape[1] // members, density.shape[2], density.shape[3])
        in_specs = (
            P("grid", "space", None, None),
            P("grid", "space", None, None),
            P("grid", None),
            P("grid"),
        )
        out_specs = P("grid", "space", None, None)
        body = functools.partial(local, plan)
        return jax.shard_map(body, mesh=mesh, in_specs=in_specs, out_specs=out_specs, check_vma=False)(density, kappa, levels, coefs)

    return whole
```

```python
import functools

import jax
import jax.numpy as jnp
import numpy as np
from jax import lax
from jax.experimental import pallas as pl
from jax.experimental.pallas import tpu as pltpu
from jax.sharding import PartitionSpec as P

ITERS = 8
BASE = 3
EXTRA = 3
TOP = BASE + EXTRA
LANES = 128
UNROLL = 8
VMEM_LIMIT = 56 * 1024 * 1024


def trailing_zeros(index):
    return (index & -index).bit_length() - 1


def level_of(index, count):
    return 0 if index == 0 else count.bit_length() - 1 - trailing_zeros(index)


def excess_of(index, count):
    return max(level_of(index, count) - BASE, 0)


def kept_indices(count):
    kept = [i for i in range(count) if level_of(i, count) <= TOP]
    return sorted(kept, key=lambda i: (excess_of(i, count), i))


def matrices(count):
    depth = count.bit_length() - 1
    hier = np.eye(count)
    dehier = np.eye(count)
    for index in range(1, count):
        spacing = 1 << trailing_zeros(index)
        hier[index, (index - spacing) % count] -= 0.5
        hier[index, (index + spacing) % count] -= 0.5
    for trailing in range(depth - 1, -1, -1):
        spacing = 1 << trailing
        for index in range(spacing, count, 2 * spacing):
            dehier[index] += 0.5 * (dehier[(index - spacing) % count] + dehier[(index + spacing) % count])
    return hier, dehier


def axis_tables(width_y, width_z):
    hier_y, dehier_y = matrices(width_y)
    hier_z, dehier_z = matrices(width_z)
    kept_y, kept_z = kept_indices(width_y), kept_indices(width_z)
    groups = width_y // 8
    order = [s * groups + j for j in range(groups) for s in range(8)]
    hy = hier_y[kept_y][:, order]
    dy = dehier_y[:, kept_y]
    hz = np.zeros((width_z, LANES))
    hz[:, : len(kept_z)] = hier_z[kept_z].T
    dz = np.zeros((LANES, width_z))
    dz[: len(kept_z)] = dehier_z[:, kept_z].T
    level_y = np.array([level_of(i, width_y) for i in kept_y])
    level_z = np.full(LANES, 99)
    level_z[: len(kept_z)] = [level_of(i, width_z) for i in kept_z]
    shape = (len(kept_y), LANES)
    ly = np.broadcast_to(level_y[:, None], shape).astype(np.int32)
    lz = np.broadcast_to(level_z[None, :], shape).astype(np.int32)
    as_bf16 = lambda m: jnp.asarray(m, jnp.bfloat16)
    return as_bf16(hy), as_bf16(hz), as_bf16(dy), as_bf16(dz), jnp.asarray(ly), jnp.asarray(lz)


class Plan:
    def __init__(self, members, slab, width_y, width_z):
        width_x = members * slab
        self.members = members
        self.stride = max(1, width_x >> TOP)
        self.rows = slab // self.stride
        kept_y = kept_indices(width_y)
        kept_z = kept_indices(width_z)
        self.blocks = len(kept_y) // 8
        block_excess = [max(excess_of(i, width_y) for i in kept_y[8 * q : 8 * q + 8]) for q in range(self.blocks)]
        width_of = [sum(excess_of(i, width_z) <= e for i in kept_z) for e in range(EXTRA + 1)]
        indices = [p * slab for p in range(members)] + [k * self.stride for k in range(1, self.rows)]
        self.levels = [level_of(i, width_x) for i in indices]
        pieces = []
        for row, index in enumerate(indices):
            for q in range(self.blocks):
                left = EXTRA - excess_of(index, width_x) - block_excess[q]
                if left >= 0:
                    pieces.append((width_of[left], row, q))
        pieces.sort(key=lambda piece: (-piece[0], piece[1], piece[2]))
        self.pieces, at = [], 0
        for width, row, q in pieces:
            if at % LANES + width > LANES:
                at += LANES - at % LANES
            self.pieces.append((row, q, at // LANES, at % LANES))
            at += width
        self.tiles = -(-at // LANES)


def split_dot(left, right, exact_left):
    value = right if exact_left else left
    high = value.astype(jnp.bfloat16)
    low = (value - high.astype(jnp.float32)).astype(jnp.bfloat16)
    dot = functools.partial(jnp.dot, preferred_element_type=jnp.float32)
    if exact_left:
        return dot(left, high) + dot(left, low)
    return dot(high, right) + dot(low, right)


def next_lane(v):
    return pltpu.roll(v, LANES - 1, 1)


def last_lane(v):
    return pltpu.roll(v, 1, 1)


def row_update(f, above, flux_below, fx, fy, fz, groups):
    gx = [fx[j] * (above[j] - f[j]) for j in range(groups)]
    follow = f[1:] + [pltpu.roll(f[0], 7, 0)]
    gy = [fy[j] * (follow[j] - f[j]) for j in range(groups)]
    before = [pltpu.roll(gy[-1], 1, 0)] + gy[:-1]
    new = []
    for j in range(groups):
        gz = fz[j] * (next_lane(f[j]) - f[j])
        plus = (f[j] + gx[j]) + (gy[j] + gz)
        minus = (flux_below[j] + before[j]) + last_lane(gz)
        new.append(plus - minus)
    return new, gx


def diffuse_kernel(plan, slab, groups, chunk, dens, kap, dprev, kprev, dnext, knext, hy, hz, out, raw_d, raw_k, f_a, f_b, fx, fy, fz, sems):
    halo = ITERS
    chunks = slab // chunk
    copies = []
    for c in range(chunks):
        part = pl.ds(c * chunk, chunk)
        pair = (
            pltpu.make_async_copy(kap.at[0, part], raw_k.at[part], sems.at[0, c]),
            pltpu.make_async_copy(dens.at[0, part], raw_d.at[part], sems.at[1, c]),
        )
        for copy in pair:
            copy.start()
        copies.append(pair)

    def natural(ref, row):
        return [ref[row, pl.ds(j, 8, stride=groups), :] for j in range(groups)]

    def stored(ref, row):
        return [ref[row, j] for j in range(groups)]

    def put(ref, row, values):
        for j in range(groups):
            ref[row, j] = values[j]

    def first(r, k_above, d_above, carry):
        k, d, flux = carry
        x_face = [0.5 * (k[j] + k_above[j]) for j in range(groups)]
        k_next = k[1:] + [pltpu.roll(k[0], 7, 0)]
        y_face = [0.5 * (k[j] + k_next[j]) for j in range(groups)]
        z_face = [0.5 * (k[j] + next_lane(k[j])) for j in range(groups)]
        put(fx, r - 1, x_face)
        put(fy, r - 1, y_face)
        put(fz, r - 1, z_face)
        new, flux = row_update(d, d_above, flux, x_face, y_face, z_face, groups)
        put(f_a, r - 1, new)
        return k_above, d_above, flux

    zero = [jnp.zeros((8, LANES), jnp.float32)] * groups
    carry = (natural(kprev, 0), natural(dprev, 0), zero)
    for r in range(1, halo):
        carry = first(r, natural(kprev, r), natural(dprev, r), carry)
    for c in range(chunks):
        for copy in copies[c]:
            copy.wait()

        def several(i, carry, c=c):
            for u in range(UNROLL):
                x = c * chunk + i * UNROLL + u
                carry = first(x + halo, natural(raw_k, x), natural(raw_d, x), carry)
            return carry

        carry = lax.fori_loop(0, chunk // UNROLL, several, carry)
    first(slab + halo, natural(knext, 0), natural(dnext, 0), carry)

    stride = plan.stride
    left = ITERS - 2
    old, new_f = f_a, f_b
    while 2 * left + 1 >= stride:
        low, high = halo - left, halo + slab - stride + left
        count, rest = (high - low + 1) // UNROLL, (high - low + 1) % UNROLL

        def one(r, carry, old=old, new_f=new_f):
            row, flux = carry
            above = stored(old, r + 1)
            new, flux = row_update(row, above, flux, stored(fx, r), stored(fy, r), stored(fz, r), groups)
            put(new_f, r, new)
            return above, flux

        def several_steps(i, carry, low=low, one=one):
            for u in range(UNROLL):
                carry = one(low + UNROLL * i + u, carry)
            return carry

        row = stored(old, low)
        below = stored(old, low - 1)
        face = stored(fx, low - 1)
        flux = [face[j] * (row[j] - below[j]) for j in range(groups)]
        carry = lax.fori_loop(0, count, several_steps, (row, flux))
        for r in range(low + UNROLL * count, high + 1):
            carry = one(r, carry)
        old, new_f = new_f, old
        left -= 1

    def cone_step(center, wanted, reach, old, new_f):
        def near(j, far):
            return any(min((j - w) % groups, (w - j) % groups) <= far for w in wanted)

        flux = {}
        for offset in range(-reach, reach + 1):
            need = [j for j in range(groups) if near(j, reach - abs(offset))]
            r = center + offset
            cells = {}

            def cell(j):
                if j not in cells:
                    cells[j] = old[r, j]
                return cells[j]

            below, flux, fluxes_y = flux, {}, {}

            def flux_y(j):
                if j not in fluxes_y:
                    follow = cell(j + 1) if j + 1 < groups else pltpu.roll(cell(0), 7, 0)
                    fluxes_y[j] = fy[r, j] * (follow - cell(j))
                return fluxes_y[j]

            for j in need:
                here = cell(j)
                flux[j] = fx[r, j] * (old[r + 1, j] - here)
                lower = below[j] if j in below else fx[r - 1, j] * (here - old[r - 1, j])
                before = flux_y(j - 1) if j else pltpu.roll(flux_y(groups - 1), 1, 0)
                gz = fz[r, j] * (next_lane(here) - here)
                new_f[r, j] = ((here + flux[j]) + (flux_y(j) + gz)) - ((lower + before) + last_lane(gz))

    period = min(8, plan.rows)

    def cones(i, _):
        source, target = old, new_f
        for reach in range(left, -1, -1):
            for k in range(period):
                spare = EXTRA if k == 0 else min(EXTRA, trailing_zeros(k))
                step = max(1, groups >> spare)
                center = halo + (i * period + k) * stride
                cone_step(center, list(range(0, groups, step)), reach, source, target)
            source, target = target, source
        return 0

    lax.fori_loop(0, plan.rows // period, cones, 0)
    done = old if left % 2 else new_f

    for k in range(plan.rows):
        plane = done[halo + k * stride].reshape(groups * 8, LANES)
        out[k] = split_dot(split_dot(hy[...], plane, True), hz[...], False)


def grid_mask(levels, ly, lz):
    return (ly[...] <= levels[0, 1]) & (lz[...] <= levels[0, 2])


def pack_kernel(plan, pos_ref, levels, coefs, ly, lz, planes, coarse, out):
    mask = grid_mask(levels, ly, lz)
    weight = coefs[0].astype(jnp.float32)
    members, rows = plan.members, plan.rows
    surplus = []
    for p in range(members):
        if p == 0:
            value = coarse[0]
        else:
            h = 1 << trailing_zeros(p)
            value = coarse[p] - 0.5 * (coarse[p - h] + coarse[(p + h) % members])
        surplus.append(value)
    following = coarse[lax.rem(pos_ref[0] + 1, members)]
    for k in range(1, rows):
        h = 1 << trailing_zeros(k)
        above = planes[k + h] if k + h < rows else following
        surplus.append(planes[k] - 0.5 * (planes[k - h] + above))
    for row in range(len(surplus)):
        scale = jnp.where(plan.levels[row] <= levels[0, 0], weight, 0.0)
        surplus[row] = jnp.where(mask, scale * surplus[row], 0.0)
    tiles = [None] * plan.tiles
    for row, q, tile, lane in plan.pieces:
        piece = surplus[row][8 * q : 8 * q + 8]
        if lane:
            piece = pltpu.roll(piece, lane, 1)
        tiles[tile] = piece if tiles[tile] is None else tiles[tile] + piece
    for tile in range(plan.tiles):
        out[tile] = tiles[tile]


def expand_kernel(plan, slab, pos_ref, levels, ly, lz, dy, dz, packed, out, coarse, nodes, buf, sems):
    mask = grid_mask(levels, ly, lz)
    members, rows, stride = plan.members, plan.rows, plan.stride
    where = {(row, q): (tile, lane) for row, q, tile, lane in plan.pieces}

    def total(row):
        parts = []
        for q in range(plan.blocks):
            if (row, q) in where:
                tile, lane = where[row, q]
                piece = packed[tile]
                if lane:
                    piece = pltpu.roll(piece, LANES - lane, 1)
                keep = mask[8 * q : 8 * q + 8] & (plan.levels[row] <= levels[0, 0])
                parts.append(jnp.where(keep, piece, 0.0))
            else:
                parts.append(jnp.zeros((8, LANES), jnp.float32))
        return jnp.concatenate(parts, axis=0)

    values = [total(p) for p in range(members)]
    h = members // 2
    while h:
        for p in range(h, members, 2 * h):
            values[p] = values[p] + 0.5 * (values[p - h] + values[(p + h) % members])
        h //= 2
    for p in range(members):
        coarse[p] = values[p]
    pos = pos_ref[0]
    fine = [coarse[pos]] + [total(members + k - 1) for k in range(1, rows)] + [coarse[lax.rem(pos + 1, members)]]
    h = rows // 2
    while h:
        for k in range(h, rows, 2 * h):
            fine[k] = fine[k] + 0.5 * (fine[k - h] + fine[k + h])
        h //= 2
    for k in range(rows + 1):
        nodes[k] = split_dot(dy[...], split_dot(fine[k], dz[...], False), True)

    def chunk(k):
        part = pl.ds(k * stride, stride)
        return pltpu.make_async_copy(buf.at[part], out.at[0, part], sems.at[k])

    def fill(k, _):
        here = nodes[k]
        step = (nodes[k + 1] - here) * (1.0 / stride)
        for j in range(stride):
            buf[k * stride + j] = here + float(j) * step if j else here
        chunk(k).start()
        return 0

    lax.fori_loop(0, rows, fill, 0)

    def drain(k, _):
        chunk(k).wait()
        return 0

    lax.fori_loop(0, rows, drain, 0)


def local(plan, density, kappa, levels, coefs):
    _, slab, width_y, width_z = density.shape
    groups = width_y // 8
    members = lax.axis_size("space")
    position = lax.axis_index("space")
    hy, hz, dy, dz, ly, lz = axis_tables(width_y, width_z)
    pos = jnp.reshape(position, (1,)).astype(jnp.int32)
    up = [(i, (i + 1) % members) for i in range(members)]
    down = [(j, i) for i, j in up]
    dprev = lax.ppermute(density[0, slab - ITERS :], "space", up)
    kprev = lax.ppermute(kappa[0, slab - ITERS :], "space", up)
    dnext = lax.ppermute(density[0, :1], "space", down)
    knext = lax.ppermute(kappa[0, :1], "space", down)

    vmem = pl.BlockSpec(memory_space=pltpu.VMEM)
    smem = pl.BlockSpec(memory_space=pltpu.SMEM)
    anywhere = pl.BlockSpec(memory_space=pl.ANY)
    params = pltpu.CompilerParams(vmem_limit_bytes=VMEM_LIMIT)
    kept = ly.shape[0]
    chunk = min(32, slab)
    extended = pltpu.VMEM((slab + ITERS, groups, 8, LANES), jnp.float32)
    raw = pltpu.VMEM((slab, width_y, width_z), jnp.float32)
    planes = pl.pallas_call(
        functools.partial(diffuse_kernel, plan, slab, groups, chunk),
        out_shape=jax.ShapeDtypeStruct((plan.rows, kept, LANES), jnp.float32),
        in_specs=[anywhere, anywhere] + [vmem] * 6,
        out_specs=vmem,
        scratch_shapes=[raw, raw, extended, extended, extended, extended, extended, pltpu.SemaphoreType.DMA((2, slab // chunk))],
        compiler_params=params,
        name="diffuse",
    )(density, kappa, dprev, kprev, dnext, knext, hy, hz)

    coarse = lax.all_gather(planes[0], "space", axis=0)
    packed = pl.pallas_call(
        functools.partial(pack_kernel, plan),
        out_shape=jax.ShapeDtypeStruct((plan.tiles, 8, LANES), jnp.float32),
        in_specs=[smem, smem, smem] + [vmem] * 4,
        out_specs=vmem,
        compiler_params=params,
        name="pack",
    )(pos, levels, coefs, ly, lz, planes, coarse)

    packed = lax.psum(packed, "grid")

    return pl.pallas_call(
        functools.partial(expand_kernel, plan, slab),
        out_shape=jax.ShapeDtypeStruct(density.shape, jnp.float32),
        in_specs=[smem, smem] + [vmem] * 5,
        out_specs=anywhere,
        scratch_shapes=[
            pltpu.VMEM((plan.members, kept, LANES), jnp.float32),
            pltpu.VMEM((plan.rows + 1, width_y, width_z), jnp.float32),
            raw,
            pltpu.SemaphoreType.DMA((plan.rows,)),
        ],
        compiler_params=params,
        name="expand",
    )(pos, levels, ly, lz, dy, dz, packed)


def solution(mesh):
    def whole(density, kappa, levels, coefs):
        members = mesh.shape["space"]
        plan = Plan(members, density.shape[1] // members, density.shape[2], density.shape[3])
        in_specs = (
            P("grid", "space", None, None),
            P("grid", "space", None, None),
            P("grid", None),
            P("grid"),
        )
        out_specs = P("grid", "space", None, None)
        body = functools.partial(local, plan)
        return jax.shard_map(body, mesh=mesh, in_specs=in_specs, out_specs=out_specs, check_vma=False)(density, kappa, levels, coefs)

    return whole
```

```python
import functools

import jax
import jax.numpy as jnp
import numpy as np
from jax import lax
from jax.experimental import pallas as pl
from jax.experimental.pallas import tpu as pltpu
from jax.sharding import PartitionSpec as P

ITERS = 8
BASE = 3
EXTRA = 3
TOP = BASE + EXTRA
LANES = 128
UNROLL = 8
VMEM_LIMIT = 56 * 1024 * 1024


def trailing_zeros(index):
    return (index & -index).bit_length() - 1


def level_of(index, count):
    return 0 if index == 0 else count.bit_length() - 1 - trailing_zeros(index)


def excess_of(index, count):
    return max(level_of(index, count) - BASE, 0)


def kept_indices(count):
    kept = [i for i in range(count) if level_of(i, count) <= TOP]
    return sorted(kept, key=lambda i: (excess_of(i, count), i))


def matrices(count):
    depth = count.bit_length() - 1
    hier = np.eye(count)
    dehier = np.eye(count)
    for index in range(1, count):
        spacing = 1 << trailing_zeros(index)
        hier[index, (index - spacing) % count] -= 0.5
        hier[index, (index + spacing) % count] -= 0.5
    for trailing in range(depth - 1, -1, -1):
        spacing = 1 << trailing
        for index in range(spacing, count, 2 * spacing):
            dehier[index] += 0.5 * (dehier[(index - spacing) % count] + dehier[(index + spacing) % count])
    return hier, dehier


def axis_tables(width_y, width_z):
    hier_y, dehier_y = matrices(width_y)
    hier_z, dehier_z = matrices(width_z)
    kept_y, kept_z = kept_indices(width_y), kept_indices(width_z)
    groups = width_y // 8
    order = [s * groups + j for j in range(groups) for s in range(8)]
    hy = hier_y[kept_y][:, order]
    dy = dehier_y[:, kept_y]
    hz = np.zeros((width_z, LANES))
    hz[:, : len(kept_z)] = hier_z[kept_z].T
    dz = np.zeros((LANES, width_z))
    dz[: len(kept_z)] = dehier_z[:, kept_z].T
    level_y = np.array([level_of(i, width_y) for i in kept_y])
    level_z = np.full(LANES, 99)
    level_z[: len(kept_z)] = [level_of(i, width_z) for i in kept_z]
    shape = (len(kept_y), LANES)
    ly = np.broadcast_to(level_y[:, None], shape).astype(np.int32)
    lz = np.broadcast_to(level_z[None, :], shape).astype(np.int32)
    as_bf16 = lambda m: jnp.asarray(m, jnp.bfloat16)
    return as_bf16(hy), as_bf16(hz), as_bf16(dy), as_bf16(dz), jnp.asarray(ly), jnp.asarray(lz)


class Plan:
    def __init__(self, members, slab, width_y, width_z):
        width_x = members * slab
        self.members = members
        self.stride = max(1, width_x >> TOP)
        self.rows = slab // self.stride
        kept_y = kept_indices(width_y)
        kept_z = kept_indices(width_z)
        self.blocks = len(kept_y) // 8
        block_excess = [max(excess_of(i, width_y) for i in kept_y[8 * q : 8 * q + 8]) for q in range(self.blocks)]
        width_of = [sum(excess_of(i, width_z) <= e for i in kept_z) for e in range(EXTRA + 1)]
        indices = [p * slab for p in range(members)] + [k * self.stride for k in range(1, self.rows)]
        self.levels = [level_of(i, width_x) for i in indices]
        pieces = []
        for row, index in enumerate(indices):
            for q in range(self.blocks):
                left = EXTRA - excess_of(index, width_x) - block_excess[q]
                if left >= 0:
                    pieces.append((width_of[left], row, q))
        pieces.sort(key=lambda piece: (-piece[0], piece[1], piece[2]))
        self.pieces, at = [], 0
        for width, row, q in pieces:
            if at % LANES + width > LANES:
                at += LANES - at % LANES
            self.pieces.append((row, q, at // LANES, at % LANES))
            at += width
        self.tiles = -(-at // LANES)


def split_dot(left, right, exact_left):
    value = right if exact_left else left
    high = value.astype(jnp.bfloat16)
    low = (value - high.astype(jnp.float32)).astype(jnp.bfloat16)
    dot = functools.partial(jnp.dot, preferred_element_type=jnp.float32)
    if exact_left:
        return dot(left, high) + dot(left, low)
    return dot(high, right) + dot(low, right)


def next_lane(v):
    return pltpu.roll(v, LANES - 1, 1)


def last_lane(v):
    return pltpu.roll(v, 1, 1)


def row_update(f, above, flux_below, fx, fy, fz, groups):
    gx = [fx[j] * (above[j] - f[j]) for j in range(groups)]
    follow = f[1:] + [pltpu.roll(f[0], 7, 0)]
    gy = [fy[j] * (follow[j] - f[j]) for j in range(groups)]
    before = [pltpu.roll(gy[-1], 1, 0)] + gy[:-1]
    new = []
    for j in range(groups):
        gz = fz[j] * (next_lane(f[j]) - f[j])
        plus = (f[j] + gx[j]) + (gy[j] + gz)
        minus = (flux_below[j] + before[j]) + last_lane(gz)
        new.append(plus - minus)
    return new, gx


def diffuse_kernel(plan, slab, groups, chunk, dens, kap, dprev, kprev, dnext, knext, hy, hz, out, raw_d, raw_k, f_a, f_b, fx, fy, fz, sems):
    halo = ITERS
    chunks = slab // chunk
    copies = []
    for c in range(chunks):
        part = pl.ds(c * chunk, chunk)
        pair = (
            pltpu.make_async_copy(kap.at[0, part], raw_k.at[part], sems.at[0, c]),
            pltpu.make_async_copy(dens.at[0, part], raw_d.at[part], sems.at[1, c]),
        )
        for copy in pair:
            copy.start()
        copies.append(pair)

    def natural(ref, row):
        return [ref[row, pl.ds(j, 8, stride=groups), :] for j in range(groups)]

    def stored(ref, row):
        return [ref[row, j] for j in range(groups)]

    def put(ref, row, values):
        for j in range(groups):
            ref[row, j] = values[j]

    def first(r, k_above, d_above, carry):
        k, d, flux = carry
        x_face = [0.5 * (k[j] + k_above[j]) for j in range(groups)]
        k_next = k[1:] + [pltpu.roll(k[0], 7, 0)]
        y_face = [0.5 * (k[j] + k_next[j]) for j in range(groups)]
        z_face = [0.5 * (k[j] + next_lane(k[j])) for j in range(groups)]
        put(fx, r - 1, x_face)
        put(fy, r - 1, y_face)
        put(fz, r - 1, z_face)
        new, flux = row_update(d, d_above, flux, x_face, y_face, z_face, groups)
        put(f_a, r - 1, new)
        return k_above, d_above, flux

    zero = [jnp.zeros((8, LANES), jnp.float32)] * groups
    carry = (natural(kprev, 0), natural(dprev, 0), zero)
    for r in range(1, halo):
        carry = first(r, natural(kprev, r), natural(dprev, r), carry)
    for c in range(chunks):
        for copy in copies[c]:
            copy.wait()

        def several(i, carry, c=c):
            for u in range(UNROLL):
                x = c * chunk + i * UNROLL + u
                carry = first(x + halo, natural(raw_k, x), natural(raw_d, x), carry)
            return carry

        carry = lax.fori_loop(0, chunk // UNROLL, several, carry)
    first(slab + halo, natural(knext, 0), natural(dnext, 0), carry)

    stride = plan.stride
    left = ITERS - 2
    old, new_f = f_a, f_b
    while 2 * left + 1 >= stride:
        low, high = halo - left, halo + slab - stride + left
        count, rest = (high - low + 1) // UNROLL, (high - low + 1) % UNROLL

        def one(r, carry, old=old, new_f=new_f):
            row, flux = carry
            above = stored(old, r + 1)
            new, flux = row_update(row, above, flux, stored(fx, r), stored(fy, r), stored(fz, r), groups)
            put(new_f, r, new)
            return above, flux

        def several_steps(i, carry, low=low, one=one):
            for u in range(UNROLL):
                carry = one(low + UNROLL * i + u, carry)
            return carry

        row = stored(old, low)
        below = stored(old, low - 1)
        face = stored(fx, low - 1)
        flux = [face[j] * (row[j] - below[j]) for j in range(groups)]
        carry = lax.fori_loop(0, count, several_steps, (row, flux))
        for r in range(low + UNROLL * count, high + 1):
            carry = one(r, carry)
        old, new_f = new_f, old
        left -= 1

    def cone_step(center, wanted, reach, old, new_f):
        def near(j, far):
            return any(min((j - w) % groups, (w - j) % groups) <= far for w in wanted)

        flux = {}
        for offset in range(-reach, reach + 1):
            need = [j for j in range(groups) if near(j, reach - abs(offset))]
            r = center + offset
            cells = {}

            def cell(j):
                if j not in cells:
                    cells[j] = old[r, j]
                return cells[j]

            below, flux, fluxes_y = flux, {}, {}

            def flux_y(j):
                if j not in fluxes_y:
                    follow = cell(j + 1) if j + 1 < groups else pltpu.roll(cell(0), 7, 0)
                    fluxes_y[j] = fy[r, j] * (follow - cell(j))
                return fluxes_y[j]

            for j in need:
                here = cell(j)
                flux[j] = fx[r, j] * (old[r + 1, j] - here)
                lower = below[j] if j in below else fx[r - 1, j] * (here - old[r - 1, j])
                before = flux_y(j - 1) if j else pltpu.roll(flux_y(groups - 1), 1, 0)
                gz = fz[r, j] * (next_lane(here) - here)
                new_f[r, j] = ((here + flux[j]) + (flux_y(j) + gz)) - ((lower + before) + last_lane(gz))

    period = min(8, plan.rows)

    def cones(i, _):
        source, target = old, new_f
        for reach in range(left, -1, -1):
            for k in range(period):
                spare = EXTRA if k == 0 else min(EXTRA, trailing_zeros(k))
                step = max(1, groups >> spare)
                center = halo + (i * period + k) * stride
                cone_step(center, list(range(0, groups, step)), reach, source, target)
            source, target = target, source
        return 0

    lax.fori_loop(0, plan.rows // period, cones, 0)
    done = old if left % 2 else new_f

    for k in range(plan.rows):
        plane = done[halo + k * stride].reshape(groups * 8, LANES)
        out[k] = split_dot(split_dot(hy[...], plane, True), hz[...], False)


def grid_mask(levels, ly, lz):
    return (ly[...] <= levels[0, 1]) & (lz[...] <= levels[0, 2])


def combine_kernel(plan, grids, levels, coefs, ly, lz, planes, out, coarse, mine, pair, parts, send_sems, recv_sems):
    members, rows = plan.members, plan.rows
    here = lax.axis_index("space")
    grid = lax.axis_index("grid")
    partner = grid + 1 - 2 * lax.rem(grid, 2)
    space_peers = [{"space": lax.rem(here + d, members)} for d in range(1, members)]
    grid_peers = [{"grid": partner}] + [{"grid": lax.rem(grid + 2 * d, grids)} for d in range(1, grids // 2)]
    peers = space_peers + grid_peers

    barrier = pltpu.get_barrier_semaphore()
    for peer in peers:
        pl.semaphore_signal(barrier, inc=1, device_id=peer, device_id_type=pl.DeviceIdType.MESH)
    pl.semaphore_wait(barrier, len(peers))

    def remote(source, target, number):
        return pltpu.make_async_remote_copy(
            src_ref=source,
            dst_ref=target,
            send_sem=send_sems.at[number],
            recv_sem=recv_sems.at[number],
            device_id=peers[number],
            device_id_type=pl.DeviceIdType.MESH,
        )

    gathers = [remote(planes.at[0], coarse.at[here], i) for i in range(members - 1)]
    for copy in gathers:
        copy.start()
    coarse[here] = planes[0]

    mask = grid_mask(levels, ly, lz)
    weight = coefs[0].astype(jnp.float32)
    fine = {}
    for k in range(1, rows):
        h = 1 << trailing_zeros(k)
        fine[k] = planes[k] - 0.5 * planes[k - h]
        if k + h < rows:
            fine[k] = fine[k] - 0.5 * planes[k + h]
    for copy in gathers:
        copy.wait_recv()
    surplus = []
    for p in range(members):
        value = coarse[p]
        if p:
            h = 1 << trailing_zeros(p)
            value = value - 0.5 * (coarse[p - h] + coarse[(p + h) % members])
        surplus.append(value)
    following = coarse[lax.rem(here + 1, members)]
    for k in range(1, rows):
        value = fine[k]
        if k + (1 << trailing_zeros(k)) == rows:
            value = value - 0.5 * following
        surplus.append(value)
    for row in range(len(surplus)):
        scale = jnp.where(plan.levels[row] <= levels[0, 0], weight, 0.0)
        surplus[row] = jnp.where(mask, scale * surplus[row], 0.0)
    tiles = [None] * plan.tiles
    for row, q, tile, lane in plan.pieces:
        piece = surplus[row][8 * q : 8 * q + 8]
        if lane:
            piece = pltpu.roll(piece, lane, 1)
        tiles[tile] = piece if tiles[tile] is None else tiles[tile] + piece
    for tile in range(plan.tiles):
        mine[tile] = tiles[tile]

    swap = remote(mine, parts.at[0], members - 1)
    swap.start()
    swap.wait_recv()
    pair[...] = mine[...] + parts[0]
    spreads = [remote(pair, parts.at[i], members - 1 + i) for i in range(1, grids // 2)]
    for copy in spreads:
        copy.start()
    total = pair[...]
    for i, copy in enumerate(spreads):
        copy.wait_recv()
        total = total + parts[i + 1]
    out[...] = total
    for copy in gathers + [swap] + spreads:
        copy.wait_send()


def expand_kernel(plan, slab, pos_ref, levels, ly, lz, dy, dz, packed, out, coarse, nodes, buf, sems):
    mask = grid_mask(levels, ly, lz)
    members, rows, stride = plan.members, plan.rows, plan.stride
    where = {(row, q): (tile, lane) for row, q, tile, lane in plan.pieces}

    def total(row):
        parts = []
        for q in range(plan.blocks):
            if (row, q) in where:
                tile, lane = where[row, q]
                piece = packed[tile]
                if lane:
                    piece = pltpu.roll(piece, LANES - lane, 1)
                keep = mask[8 * q : 8 * q + 8] & (plan.levels[row] <= levels[0, 0])
                parts.append(jnp.where(keep, piece, 0.0))
            else:
                parts.append(jnp.zeros((8, LANES), jnp.float32))
        return jnp.concatenate(parts, axis=0)

    values = [total(p) for p in range(members)]
    h = members // 2
    while h:
        for p in range(h, members, 2 * h):
            values[p] = values[p] + 0.5 * (values[p - h] + values[(p + h) % members])
        h //= 2
    for p in range(members):
        coarse[p] = values[p]
    pos = pos_ref[0]
    fine = [coarse[pos]] + [total(members + k - 1) for k in range(1, rows)] + [coarse[lax.rem(pos + 1, members)]]
    h = rows // 2
    while h:
        for k in range(h, rows, 2 * h):
            fine[k] = fine[k] + 0.5 * (fine[k - h] + fine[k + h])
        h //= 2
    for k in range(rows + 1):
        nodes[k] = split_dot(dy[...], split_dot(fine[k], dz[...], False), True)

    def chunk(k):
        part = pl.ds(k * stride, stride)
        return pltpu.make_async_copy(buf.at[part], out.at[0, part], sems.at[k])

    def fill(k, _):
        here = nodes[k]
        step = (nodes[k + 1] - here) * (1.0 / stride)
        for j in range(stride):
            buf[k * stride + j] = here + float(j) * step if j else here
        chunk(k).start()
        return 0

    lax.fori_loop(0, rows, fill, 0)

    def drain(k, _):
        chunk(k).wait()
        return 0

    lax.fori_loop(0, rows, drain, 0)


def local(plan, density, kappa, levels, coefs):
    _, slab, width_y, width_z = density.shape
    groups = width_y // 8
    members = lax.axis_size("space")
    position = lax.axis_index("space")
    hy, hz, dy, dz, ly, lz = axis_tables(width_y, width_z)
    pos = jnp.reshape(position, (1,)).astype(jnp.int32)
    up = [(i, (i + 1) % members) for i in range(members)]
    down = [(j, i) for i, j in up]
    dprev = lax.ppermute(density[0, slab - ITERS :], "space", up)
    kprev = lax.ppermute(kappa[0, slab - ITERS :], "space", up)
    dnext = lax.ppermute(density[0, :1], "space", down)
    knext = lax.ppermute(kappa[0, :1], "space", down)

    vmem = pl.BlockSpec(memory_space=pltpu.VMEM)
    smem = pl.BlockSpec(memory_space=pltpu.SMEM)
    anywhere = pl.BlockSpec(memory_space=pl.ANY)
    params = pltpu.CompilerParams(vmem_limit_bytes=VMEM_LIMIT)
    kept = ly.shape[0]
    chunk = min(32, slab)
    extended = pltpu.VMEM((slab + ITERS, groups, 8, LANES), jnp.float32)
    raw = pltpu.VMEM((slab, width_y, width_z), jnp.float32)
    planes = pl.pallas_call(
        functools.partial(diffuse_kernel, plan, slab, groups, chunk),
        out_shape=jax.ShapeDtypeStruct((plan.rows, kept, LANES), jnp.float32),
        in_specs=[anywhere, anywhere] + [vmem] * 6,
        out_specs=vmem,
        scratch_shapes=[raw, raw, extended, extended, extended, extended, extended, pltpu.SemaphoreType.DMA((2, slab // chunk))],
        compiler_params=params,
        name="diffuse",
    )(density, kappa, dprev, kprev, dnext, knext, hy, hz)

    grids = lax.axis_size("grid")
    peers = members - 1 + grids // 2
    packed_shape = (plan.tiles, 8, LANES)
    packed = pl.pallas_call(
        functools.partial(combine_kernel, plan, grids),
        out_shape=jax.ShapeDtypeStruct(packed_shape, jnp.float32),
        in_specs=[smem, smem] + [vmem] * 3,
        out_specs=vmem,
        scratch_shapes=[
            pltpu.VMEM((members, kept, LANES), jnp.float32),
            pltpu.VMEM(packed_shape, jnp.float32),
            pltpu.VMEM(packed_shape, jnp.float32),
            pltpu.VMEM((grids // 2,) + packed_shape, jnp.float32),
            pltpu.SemaphoreType.DMA((peers,)),
            pltpu.SemaphoreType.DMA((peers,)),
        ],
        compiler_params=pltpu.CompilerParams(vmem_limit_bytes=VMEM_LIMIT, collective_id=0, has_side_effects=True),
        name="combine",
    )(levels, coefs, ly, lz, planes)

    return pl.pallas_call(
        functools.partial(expand_kernel, plan, slab),
        out_shape=jax.ShapeDtypeStruct(density.shape, jnp.float32),
        in_specs=[smem, smem] + [vmem] * 5,
        out_specs=anywhere,
        scratch_shapes=[
            pltpu.VMEM((plan.members, kept, LANES), jnp.float32),
            pltpu.VMEM((plan.rows + 1, width_y, width_z), jnp.float32),
            raw,
            pltpu.SemaphoreType.DMA((plan.rows,)),
        ],
        compiler_params=params,
        name="expand",
    )(pos, levels, ly, lz, dy, dz, packed)


def solution(mesh):
    def whole(density, kappa, levels, coefs):
        members = mesh.shape["space"]
        plan = Plan(members, density.shape[1] // members, density.shape[2], density.shape[3])
        in_specs = (
            P("grid", "space", None, None),
            P("grid", "space", None, None),
            P("grid", None),
            P("grid"),
        )
        out_specs = P("grid", "space", None, None)
        body = functools.partial(local, plan)
        return jax.shard_map(body, mesh=mesh, in_specs=in_specs, out_specs=out_specs, check_vma=False)(density, kappa, levels, coefs)

    return whole
```

```python
import functools

import jax
import jax.numpy as jnp
import numpy as np
from jax import lax
from jax.experimental import pallas as pl
from jax.experimental.pallas import tpu as pltpu
from jax.sharding import PartitionSpec as P

ITERS = 8
BASE = 3
EXTRA = 3
TOP = BASE + EXTRA
LANES = 128
UNROLL = 8
VMEM_LIMIT = 56 * 1024 * 1024


def trailing_zeros(index):
    return (index & -index).bit_length() - 1


def level_of(index, count):
    return 0 if index == 0 else count.bit_length() - 1 - trailing_zeros(index)


def excess_of(index, count):
    return max(level_of(index, count) - BASE, 0)


def kept_indices(count):
    kept = [i for i in range(count) if level_of(i, count) <= TOP]
    return sorted(kept, key=lambda i: (excess_of(i, count), i))


def matrices(count):
    depth = count.bit_length() - 1
    hier = np.eye(count)
    dehier = np.eye(count)
    for index in range(1, count):
        spacing = 1 << trailing_zeros(index)
        hier[index, (index - spacing) % count] -= 0.5
        hier[index, (index + spacing) % count] -= 0.5
    for trailing in range(depth - 1, -1, -1):
        spacing = 1 << trailing
        for index in range(spacing, count, 2 * spacing):
            dehier[index] += 0.5 * (dehier[(index - spacing) % count] + dehier[(index + spacing) % count])
    return hier, dehier


def axis_tables(width_y, width_z):
    hier_y, dehier_y = matrices(width_y)
    hier_z, dehier_z = matrices(width_z)
    kept_y, kept_z = kept_indices(width_y), kept_indices(width_z)
    groups = width_y // 8
    order = [s * groups + j for j in range(groups) for s in range(8)]
    hy = hier_y[kept_y][:, order]
    dy = dehier_y[:, kept_y]
    hz = np.zeros((width_z, LANES))
    hz[:, : len(kept_z)] = hier_z[kept_z].T
    dz = np.zeros((LANES, width_z))
    dz[: len(kept_z)] = dehier_z[:, kept_z].T
    level_y = np.array([level_of(i, width_y) for i in kept_y])
    level_z = np.full(LANES, 99)
    level_z[: len(kept_z)] = [level_of(i, width_z) for i in kept_z]
    shape = (len(kept_y), LANES)
    ly = np.broadcast_to(level_y[:, None], shape).astype(np.int32)
    lz = np.broadcast_to(level_z[None, :], shape).astype(np.int32)
    as_bf16 = lambda m: jnp.asarray(m, jnp.bfloat16)
    return as_bf16(hy), as_bf16(hz), as_bf16(dy), as_bf16(dz), jnp.asarray(ly), jnp.asarray(lz)


class Plan:
    def __init__(self, members, slab, width_y, width_z):
        width_x = members * slab
        self.members = members
        self.stride = max(1, width_x >> TOP)
        self.rows = slab // self.stride
        kept_y = kept_indices(width_y)
        kept_z = kept_indices(width_z)
        self.blocks = len(kept_y) // 8
        block_excess = [max(excess_of(i, width_y) for i in kept_y[8 * q : 8 * q + 8]) for q in range(self.blocks)]
        width_of = [sum(excess_of(i, width_z) <= e for i in kept_z) for e in range(EXTRA + 1)]
        indices = [p * slab for p in range(members)] + [k * self.stride for k in range(1, self.rows)]
        self.levels = [level_of(i, width_x) for i in indices]
        pieces = []
        for row, index in enumerate(indices):
            for q in range(self.blocks):
                left = EXTRA - excess_of(index, width_x) - block_excess[q]
                if left >= 0:
                    pieces.append((width_of[left], row, q))
        pieces.sort(key=lambda piece: (-piece[0], piece[1], piece[2]))
        self.pieces, at = [], 0
        for width, row, q in pieces:
            if at % LANES + width > LANES:
                at += LANES - at % LANES
            self.pieces.append((row, q, at // LANES, at % LANES))
            at += width
        self.tiles = -(-at // LANES)


def split_dot(left, right, exact_left):
    value = right if exact_left else left
    high = value.astype(jnp.bfloat16)
    low = (value - high.astype(jnp.float32)).astype(jnp.bfloat16)
    dot = functools.partial(jnp.dot, preferred_element_type=jnp.float32)
    if exact_left:
        return dot(left, high) + dot(left, low)
    return dot(high, right) + dot(low, right)


def next_lane(v):
    return pltpu.roll(v, LANES - 1, v.ndim - 1)


def last_lane(v):
    return pltpu.roll(v, 1, v.ndim - 1)


def next_y(v):
    return jnp.concatenate([v[1:], pltpu.roll(v[:1], 7, 1)], axis=0)


def last_y(v):
    return jnp.concatenate([pltpu.roll(v[-1:], 1, 1), v[:-1]], axis=0)


def row_update(f, above, flux_below, fx, fy, fz):
    gx = fx * (above - f)
    gy = fy * (next_y(f) - f)
    gz = fz * (next_lane(f) - f)
    return ((f + gx) + (gy + gz)) - ((flux_below + last_y(gy)) + last_lane(gz)), gx


def diffuse_kernel(plan, slab, groups, chunk, dens, kap, hy, hz, out, raw_d, raw_k, dprev, kprev, dnext, knext, f_a, f_b, fx, fy, fz, sems, send_sems, recv_sems):
    halo = ITERS
    chunks = slab // chunk
    copies = []
    for c in range(chunks):
        part = pl.ds(c * chunk, chunk)
        pair = (
            pltpu.make_async_copy(kap.at[0, part], raw_k.at[part], sems.at[0, c]),
            pltpu.make_async_copy(dens.at[0, part], raw_d.at[part], sems.at[1, c]),
        )
        for copy in pair:
            copy.start()
        copies.append(pair)

    here = lax.axis_index("space")
    up = {"space": lax.rem(here + 1, plan.members)}
    down = {"space": lax.rem(here + plan.members - 1, plan.members)}
    barrier = pltpu.get_barrier_semaphore()
    for peer in (up, down):
        pl.semaphore_signal(barrier, inc=1, device_id=peer, device_id_type=pl.DeviceIdType.MESH)
    pl.semaphore_wait(barrier, 2)
    last, initial = pl.ds(slab - halo, halo), pl.ds(0, 1)
    sends = []
    for i, (source, target, peer) in enumerate(
        (
            (kap.at[0, last], kprev, up),
            (dens.at[0, last], dprev, up),
            (kap.at[0, initial], knext, down),
            (dens.at[0, initial], dnext, down),
        )
    ):
        copy = pltpu.make_async_remote_copy(
            src_ref=source,
            dst_ref=target,
            send_sem=send_sems.at[i],
            recv_sem=recv_sems.at[i],
            device_id=peer,
            device_id_type=pl.DeviceIdType.MESH,
        )
        copy.start()
        sends.append(copy)

    def natural(ref, row):
        return jnp.stack([ref[row, pl.ds(j, 8, stride=groups), :] for j in range(groups)], axis=0)

    def first(r, k_above, d_above, carry):
        k, d, flux = carry
        x_face = 0.5 * (k + k_above)
        y_face = 0.5 * (k + next_y(k))
        z_face = 0.5 * (k + next_lane(k))
        fx[r - 1] = x_face
        fy[r - 1] = y_face
        fz[r - 1] = z_face
        f_a[r - 1], flux = row_update(d, d_above, flux, x_face, y_face, z_face)
        return k_above, d_above, flux

    def both(x, carry):
        return first(x + halo, natural(raw_k, x), natural(raw_d, x), carry)

    zero = jnp.zeros((groups, 8, LANES), jnp.float32)
    for c in range(chunks):
        for copy in copies[c]:
            copy.wait()
        start, rest = c * chunk, chunk
        if c == 0:
            carry = (natural(raw_k, 0), natural(raw_d, 0), zero)
            start, rest = 1, chunk - 1

        def several(i, carry, start=start):
            for u in range(UNROLL):
                carry = both(start + i * UNROLL + u, carry)
            return carry

        carry = lax.fori_loop(0, rest // UNROLL, several, carry)
        for x in range(start + rest // UNROLL * UNROLL, start + rest):
            carry = both(x, carry)
    for copy in sends:
        copy.wait_recv()
    first(slab + halo, natural(knext, 0), natural(dnext, 0), carry)
    carry = (natural(kprev, 0), natural(dprev, 0), zero)
    for r in range(1, halo):
        carry = first(r, natural(kprev, r), natural(dprev, r), carry)
    carry = both(0, carry)
    f_a[halo] = f_a[halo] - carry[2]

    stride = plan.stride
    left = ITERS - 2
    old, new_f = f_a, f_b
    while 2 * left + 1 >= stride:
        low, high = halo - left, halo + slab - stride + left
        count, rest = (high - low + 1) // UNROLL, (high - low + 1) % UNROLL

        def one(r, carry, old=old, new_f=new_f):
            row, flux = carry
            above = old[r + 1]
            new_f[r], flux = row_update(row, above, flux, fx[r], fy[r], fz[r])
            return above, flux

        def several_steps(i, carry, low=low, one=one):
            for u in range(UNROLL):
                carry = one(low + UNROLL * i + u, carry)
            return carry

        row = old[low]
        flux = fx[low - 1] * (row - old[low - 1])
        carry = lax.fori_loop(0, count, several_steps, (row, flux))
        for r in range(low + UNROLL * count, high + 1):
            carry = one(r, carry)
        old, new_f = new_f, old
        left -= 1

    def cone_step(center, wanted, reach, old, new_f):
        def near(j, far):
            return any(min((j - w) % groups, (w - j) % groups) <= far for w in wanted)

        flux = {}
        for offset in range(-reach, reach + 1):
            need = [j for j in range(groups) if near(j, reach - abs(offset))]
            r = center + offset
            cells = {}

            def cell(j):
                if j not in cells:
                    cells[j] = old[r, j]
                return cells[j]

            below, flux, fluxes_y = flux, {}, {}

            def flux_y(j):
                if j not in fluxes_y:
                    follow = cell(j + 1) if j + 1 < groups else pltpu.roll(cell(0), 7, 0)
                    fluxes_y[j] = fy[r, j] * (follow - cell(j))
                return fluxes_y[j]

            for j in need:
                here = cell(j)
                flux[j] = fx[r, j] * (old[r + 1, j] - here)
                lower = below[j] if j in below else fx[r - 1, j] * (here - old[r - 1, j])
                before = flux_y(j - 1) if j else pltpu.roll(flux_y(groups - 1), 1, 0)
                gz = fz[r, j] * (next_lane(here) - here)
                new_f[r, j] = ((here + flux[j]) + (flux_y(j) + gz)) - ((lower + before) + last_lane(gz))

    period = min(8, plan.rows)

    def cones(i, _):
        source, target = old, new_f
        for reach in range(left, -1, -1):
            for k in range(period):
                spare = EXTRA if k == 0 else min(EXTRA, trailing_zeros(k))
                step = max(1, groups >> spare)
                center = halo + (i * period + k) * stride
                cone_step(center, list(range(0, groups, step)), reach, source, target)
            source, target = target, source
        return 0

    lax.fori_loop(0, plan.rows // period, cones, 0)
    done = old if left % 2 else new_f

    planes = [done[halo + k * stride].reshape(groups * 8, LANES) for k in range(plan.rows)]
    planes = split_dot(jnp.concatenate(planes, axis=0), hz[...], False)
    planes = jnp.concatenate([planes[k * groups * 8 : (k + 1) * groups * 8] for k in range(plan.rows)], axis=1)
    planes = split_dot(hy[...], planes, True)
    for k in range(plan.rows):
        out[k] = planes[:, k * LANES : (k + 1) * LANES]
    for copy in sends:
        copy.wait_send()


def grid_mask(levels, ly, lz):
    return (ly[...] <= levels[0, 1]) & (lz[...] <= levels[0, 2])


def combine_kernel(plan, grids, levels, coefs, ly, lz, planes, out, coarse, mine, pair, parts, send_sems, recv_sems):
    members, rows = plan.members, plan.rows
    here = lax.axis_index("space")
    grid = lax.axis_index("grid")
    partner = grid + 1 - 2 * lax.rem(grid, 2)
    space_peers = [{"space": lax.rem(here + d, members)} for d in range(1, members)]
    grid_peers = [{"grid": partner}] + [{"grid": lax.rem(grid + 2 * d, grids)} for d in range(1, grids // 2)]
    peers = space_peers + grid_peers

    barrier = pltpu.get_barrier_semaphore()
    for peer in peers:
        pl.semaphore_signal(barrier, inc=1, device_id=peer, device_id_type=pl.DeviceIdType.MESH)
    pl.semaphore_wait(barrier, len(peers))

    def remote(source, target, number):
        return pltpu.make_async_remote_copy(
            src_ref=source,
            dst_ref=target,
            send_sem=send_sems.at[number],
            recv_sem=recv_sems.at[number],
            device_id=peers[number],
            device_id_type=pl.DeviceIdType.MESH,
        )

    gathers = [remote(planes.at[0], coarse.at[here], i) for i in range(members - 1)]
    for copy in gathers:
        copy.start()
    coarse[here] = planes[0]

    mask = grid_mask(levels, ly, lz)
    weight = coefs[0].astype(jnp.float32)
    fine = {}
    for k in range(1, rows):
        h = 1 << trailing_zeros(k)
        fine[k] = planes[k] - 0.5 * planes[k - h]
        if k + h < rows:
            fine[k] = fine[k] - 0.5 * planes[k + h]
    for copy in gathers:
        copy.wait_recv()
    surplus = []
    for p in range(members):
        value = coarse[p]
        if p:
            h = 1 << trailing_zeros(p)
            value = value - 0.5 * (coarse[p - h] + coarse[(p + h) % members])
        surplus.append(value)
    following = coarse[lax.rem(here + 1, members)]
    for k in range(1, rows):
        value = fine[k]
        if k + (1 << trailing_zeros(k)) == rows:
            value = value - 0.5 * following
        surplus.append(value)
    for row in range(len(surplus)):
        scale = jnp.where(plan.levels[row] <= levels[0, 0], weight, 0.0)
        surplus[row] = jnp.where(mask, scale * surplus[row], 0.0)
    tiles = [None] * plan.tiles
    for row, q, tile, lane in plan.pieces:
        piece = surplus[row][8 * q : 8 * q + 8]
        if lane:
            piece = pltpu.roll(piece, lane, 1)
        tiles[tile] = piece if tiles[tile] is None else tiles[tile] + piece
    for tile in range(plan.tiles):
        mine[tile] = tiles[tile]

    swap = remote(mine, parts.at[0], members - 1)
    swap.start()
    swap.wait_recv()
    pair[...] = mine[...] + parts[0]
    spreads = [remote(pair, parts.at[i], members - 1 + i) for i in range(1, grids // 2)]
    for copy in spreads:
        copy.start()
    total = pair[...]
    for i, copy in enumerate(spreads):
        copy.wait_recv()
        total = total + parts[i + 1]
    out[...] = total
    for copy in gathers + [swap] + spreads:
        copy.wait_send()


def expand_kernel(plan, slab, pos_ref, levels, ly, lz, dy, dz, packed, out, coarse, nodes, buf, sems):
    mask = grid_mask(levels, ly, lz)
    members, rows, stride = plan.members, plan.rows, plan.stride
    where = {(row, q): (tile, lane) for row, q, tile, lane in plan.pieces}

    def total(row):
        parts = []
        for q in range(plan.blocks):
            if (row, q) in where:
                tile, lane = where[row, q]
                piece = packed[tile]
                if lane:
                    piece = pltpu.roll(piece, LANES - lane, 1)
                keep = mask[8 * q : 8 * q + 8] & (plan.levels[row] <= levels[0, 0])
                parts.append(jnp.where(keep, piece, 0.0))
            else:
                parts.append(jnp.zeros((8, LANES), jnp.float32))
        return jnp.concatenate(parts, axis=0)

    values = [total(p) for p in range(members)]
    h = members // 2
    while h:
        for p in range(h, members, 2 * h):
            values[p] = values[p] + 0.5 * (values[p - h] + values[(p + h) % members])
        h //= 2
    for p in range(members):
        coarse[p] = values[p]
    pos = pos_ref[0]
    fine = [coarse[pos]] + [total(members + k - 1) for k in range(1, rows)] + [coarse[lax.rem(pos + 1, members)]]
    h = rows // 2
    while h:
        for k in range(h, rows, 2 * h):
            fine[k] = fine[k] + 0.5 * (fine[k - h] + fine[k + h])
        h //= 2

    def chunk(k):
        part = pl.ds(k * stride, stride)
        return pltpu.make_async_copy(buf.at[part], out.at[0, part], sems.at[k])

    def fill(k, _):
        here = nodes[k]
        step = (nodes[k + 1] - here) * (1.0 / stride)
        for j in range(stride):
            buf[k * stride + j] = here + float(j) * step if j else here
        chunk(k).start()
        return 0

    def transform(low, high):
        size = fine[0].shape[0]
        part = split_dot(jnp.concatenate(fine[low:high], axis=0), dz[...], False)
        part = jnp.concatenate([part[i * size : (i + 1) * size] for i in range(high - low)], axis=1)
        part = split_dot(dy[...], part, True)
        for i in range(high - low):
            nodes[low + i] = part[:, i * LANES : (i + 1) * LANES]

    half = rows // 2
    transform(0, half + 1)
    lax.fori_loop(0, half, fill, 0)
    transform(half + 1, rows + 1)
    lax.fori_loop(half, rows, fill, 0)

    def drain(k, _):
        chunk(k).wait()
        return 0

    lax.fori_loop(0, rows, drain, 0)


def local(plan, density, kappa, levels, coefs):
    _, slab, width_y, width_z = density.shape
    groups = width_y // 8
    members = lax.axis_size("space")
    position = lax.axis_index("space")
    hy, hz, dy, dz, ly, lz = axis_tables(width_y, width_z)
    pos = jnp.reshape(position, (1,)).astype(jnp.int32)
    vmem = pl.BlockSpec(memory_space=pltpu.VMEM)
    smem = pl.BlockSpec(memory_space=pltpu.SMEM)
    anywhere = pl.BlockSpec(memory_space=pl.ANY)
    params = pltpu.CompilerParams(vmem_limit_bytes=VMEM_LIMIT)
    kept = ly.shape[0]
    chunk = min(32, slab)
    extended = pltpu.VMEM((slab + ITERS, groups, 8, LANES), jnp.float32)
    raw = pltpu.VMEM((slab, width_y, width_z), jnp.float32)
    below = pltpu.VMEM((ITERS, width_y, width_z), jnp.float32)
    above = pltpu.VMEM((1, width_y, width_z), jnp.float32)
    planes = pl.pallas_call(
        functools.partial(diffuse_kernel, plan, slab, groups, chunk),
        out_shape=jax.ShapeDtypeStruct((plan.rows, kept, LANES), jnp.float32),
        in_specs=[anywhere, anywhere, vmem, vmem],
        out_specs=vmem,
        scratch_shapes=[raw, raw, below, below, above, above]
        + [extended] * 5
        + [pltpu.SemaphoreType.DMA((2, slab // chunk)), pltpu.SemaphoreType.DMA((4,)), pltpu.SemaphoreType.DMA((4,))],
        compiler_params=pltpu.CompilerParams(vmem_limit_bytes=VMEM_LIMIT, collective_id=1, has_side_effects=True),
        name="diffuse",
    )(density, kappa, hy, hz)

    grids = lax.axis_size("grid")
    peers = members - 1 + grids // 2
    packed_shape = (plan.tiles, 8, LANES)
    packed = pl.pallas_call(
        functools.partial(combine_kernel, plan, grids),
        out_shape=jax.ShapeDtypeStruct(packed_shape, jnp.float32),
        in_specs=[smem, smem] + [vmem] * 3,
        out_specs=vmem,
        scratch_shapes=[
            pltpu.VMEM((members, kept, LANES), jnp.float32),
            pltpu.VMEM(packed_shape, jnp.float32),
            pltpu.VMEM(packed_shape, jnp.float32),
            pltpu.VMEM((grids // 2,) + packed_shape, jnp.float32),
            pltpu.SemaphoreType.DMA((peers,)),
            pltpu.SemaphoreType.DMA((peers,)),
        ],
        compiler_params=pltpu.CompilerParams(vmem_limit_bytes=VMEM_LIMIT, collective_id=0, has_side_effects=True),
        name="combine",
    )(levels, coefs, ly, lz, planes)

    return pl.pallas_call(
        functools.partial(expand_kernel, plan, slab),
        out_shape=jax.ShapeDtypeStruct(density.shape, jnp.float32),
        in_specs=[smem, smem] + [vmem] * 5,
        out_specs=anywhere,
        scratch_shapes=[
            pltpu.VMEM((plan.members, kept, LANES), jnp.float32),
            pltpu.VMEM((plan.rows + 1, width_y, width_z), jnp.float32),
            raw,
            pltpu.SemaphoreType.DMA((plan.rows,)),
        ],
        compiler_params=params,
        name="expand",
    )(pos, levels, ly, lz, dy, dz, packed)


def solution(mesh):
    def whole(density, kappa, levels, coefs):
        members = mesh.shape["space"]
        plan = Plan(members, density.shape[1] // members, density.shape[2], density.shape[3])
        in_specs = (
            P("grid", "space", None, None),
            P("grid", "space", None, None),
            P("grid", None),
            P("grid"),
        )
        out_specs = P("grid", "space", None, None)
        body = functools.partial(local, plan)
        return jax.shard_map(body, mesh=mesh, in_specs=in_specs, out_specs=out_specs, check_vma=False)(density, kappa, levels, coefs)

    return whole
```

```python
import functools

import jax
import jax.numpy as jnp
import numpy as np
from jax import lax
from jax.experimental import pallas as pl
from jax.experimental.pallas import tpu as pltpu
from jax.sharding import PartitionSpec as P

ITERS = 8
BASE = 3
EXTRA = 3
TOP = BASE + EXTRA
LANES = 128
UNROLL = 16
VMEM_LIMIT = 56 * 1024 * 1024


def trailing_zeros(index):
    return (index & -index).bit_length() - 1


def level_of(index, count):
    return 0 if index == 0 else count.bit_length() - 1 - trailing_zeros(index)


def excess_of(index, count):
    return max(level_of(index, count) - BASE, 0)


def kept_indices(count):
    kept = [i for i in range(count) if level_of(i, count) <= TOP]
    return sorted(kept, key=lambda i: (excess_of(i, count), i))


def matrices(count):
    depth = count.bit_length() - 1
    hier = np.eye(count)
    dehier = np.eye(count)
    for index in range(1, count):
        spacing = 1 << trailing_zeros(index)
        hier[index, (index - spacing) % count] -= 0.5
        hier[index, (index + spacing) % count] -= 0.5
    for trailing in range(depth - 1, -1, -1):
        spacing = 1 << trailing
        for index in range(spacing, count, 2 * spacing):
            dehier[index] += 0.5 * (dehier[(index - spacing) % count] + dehier[(index + spacing) % count])
    return hier, dehier


def axis_tables(width_y, width_z):
    hier_y, dehier_y = matrices(width_y)
    hier_z, dehier_z = matrices(width_z)
    kept_y, kept_z = kept_indices(width_y), kept_indices(width_z)
    groups = width_y // 8
    order = [s * groups + j for j in range(groups) for s in range(8)]
    hy = hier_y[kept_y][:, order]
    dy = dehier_y[:, kept_y]
    hz = np.zeros((width_z, LANES))
    hz[:, : len(kept_z)] = hier_z[kept_z].T
    dz = np.zeros((LANES, width_z))
    dz[: len(kept_z)] = dehier_z[:, kept_z].T
    level_y = np.array([level_of(i, width_y) for i in kept_y])
    level_z = np.full(LANES, 99)
    level_z[: len(kept_z)] = [level_of(i, width_z) for i in kept_z]
    shape = (len(kept_y), LANES)
    ly = np.broadcast_to(level_y[:, None], shape).astype(np.int32)
    lz = np.broadcast_to(level_z[None, :], shape).astype(np.int32)
    as_bf16 = lambda m: jnp.asarray(m, jnp.bfloat16)
    return as_bf16(hy), as_bf16(hz), as_bf16(dy), as_bf16(dz), jnp.asarray(ly), jnp.asarray(lz)


class Plan:
    def __init__(self, members, slab, width_y, width_z):
        width_x = members * slab
        self.members = members
        self.stride = max(1, width_x >> TOP)
        self.rows = slab // self.stride
        kept_y = kept_indices(width_y)
        kept_z = kept_indices(width_z)
        self.blocks = len(kept_y) // 8
        block_excess = [max(excess_of(i, width_y) for i in kept_y[8 * q : 8 * q + 8]) for q in range(self.blocks)]
        width_of = [sum(excess_of(i, width_z) <= e for i in kept_z) for e in range(EXTRA + 1)]
        indices = [p * slab for p in range(members)] + [k * self.stride for k in range(1, self.rows)]
        self.levels = [level_of(i, width_x) for i in indices]
        pieces = []
        for row, index in enumerate(indices):
            for q in range(self.blocks):
                left = EXTRA - excess_of(index, width_x) - block_excess[q]
                if left >= 0:
                    pieces.append((width_of[left], row, q))
        pieces.sort(key=lambda piece: (-piece[0], piece[1], piece[2]))
        self.pieces, at = [], 0
        for width, row, q in pieces:
            if at % LANES + width > LANES:
                at += LANES - at % LANES
            self.pieces.append((row, q, at // LANES, at % LANES))
            at += width
        self.tiles = -(-at // LANES)


def split_dot(left, right, exact_left):
    value = right if exact_left else left
    high = value.astype(jnp.bfloat16)
    low = (value - high.astype(jnp.float32)).astype(jnp.bfloat16)
    dot = functools.partial(jnp.dot, preferred_element_type=jnp.float32)
    if exact_left:
        return dot(left, high) + dot(left, low)
    return dot(high, right) + dot(low, right)


def next_lane(v):
    return pltpu.roll(v, LANES - 1, v.ndim - 1)


def last_lane(v):
    return pltpu.roll(v, 1, v.ndim - 1)


def next_y(v):
    return jnp.concatenate([v[1:], pltpu.roll(v[:1], 7, 1)], axis=0)


def last_y(v):
    return jnp.concatenate([pltpu.roll(v[-1:], 1, 1), v[:-1]], axis=0)


def row_update(f, above, flux_below, fx, fy, fz):
    gx = fx * (above - f)
    gy = fy * (next_y(f) - f)
    gz = fz * (next_lane(f) - f)
    return ((f + gx) + (gy + gz)) - ((flux_below + last_y(gy)) + last_lane(gz)), gx


def grid_mask(levels, ly, lz):
    return (ly[...] <= levels[0, 1]) & (lz[...] <= levels[0, 2])


def combine(plan, grids, here, remote, gathers, levels, coefs, ly, lz, planes, out, coarse, mine, pair, parts):
    members, rows = plan.members, plan.rows
    mask = grid_mask(levels, ly, lz)
    weight = coefs[0].astype(jnp.float32)
    fine = {}
    for k in range(1, rows):
        h = 1 << trailing_zeros(k)
        fine[k] = planes[k] - 0.5 * planes[k - h]
        if k + h < rows:
            fine[k] = fine[k] - 0.5 * planes[k + h]
    coarse[here] = planes[0]
    for copy in gathers:
        copy.wait_recv()
    surplus = []
    for p in range(members):
        value = coarse[p]
        if p:
            h = 1 << trailing_zeros(p)
            value = value - 0.5 * (coarse[p - h] + coarse[(p + h) % members])
        surplus.append(value)
    following = coarse[lax.rem(here + 1, members)]
    for k in range(1, rows):
        value = fine[k]
        if k + (1 << trailing_zeros(k)) == rows:
            value = value - 0.5 * following
        surplus.append(value)
    for row in range(len(surplus)):
        scale = jnp.where(plan.levels[row] <= levels[0, 0], weight, 0.0)
        surplus[row] = jnp.where(mask, scale * surplus[row], 0.0)
    tiles = [None] * plan.tiles
    for row, q, tile, lane in plan.pieces:
        piece = surplus[row][8 * q : 8 * q + 8]
        if lane:
            piece = pltpu.roll(piece, lane, 1)
        tiles[tile] = piece if tiles[tile] is None else tiles[tile] + piece
    for tile in range(plan.tiles):
        mine[tile] = tiles[tile]

    swap = remote(mine, parts.at[0], members - 1)
    swap.start()
    swap.wait_recv()
    pair[...] = mine[...] + parts[0]
    spreads = [remote(pair, parts.at[i], members - 1 + i) for i in range(1, grids // 2)]
    for copy in spreads:
        copy.start()
    total = pair[...]
    for i, copy in enumerate(spreads):
        copy.wait_recv()
        total = total + parts[i + 1]
    out[...] = total
    for copy in gathers + [swap] + spreads:
        copy.wait_send()


def surplus_kernel(
    plan, grids, slab, groups, chunk, levels, coefs, ly, lz, dens, kap, hy, hz, out,
    raw_d, raw_k, dprev, kprev, dnext, knext, f_a, f_b, fx, fy, fz, planes, coarse, mine, pair, parts,
    sems, halo_send, halo_recv, send_sems, recv_sems,
):
    halo = ITERS
    chunks = slab // chunk
    copies = []
    for c in range(chunks):
        part = pl.ds(c * chunk, chunk)
        both_copies = (
            pltpu.make_async_copy(kap.at[0, part], raw_k.at[part], sems.at[0, c]),
            pltpu.make_async_copy(dens.at[0, part], raw_d.at[part], sems.at[1, c]),
        )
        for copy in both_copies:
            copy.start()
        copies.append(both_copies)

    here = lax.axis_index("space")
    up = {"space": lax.rem(here + 1, plan.members)}
    down = {"space": lax.rem(here + plan.members - 1, plan.members)}
    grid = lax.axis_index("grid")
    partner = grid + 1 - 2 * lax.rem(grid, 2)
    peers = [{"space": lax.rem(here + d, plan.members)} for d in range(1, plan.members)]
    peers += [{"grid": partner}] + [{"grid": lax.rem(grid + 2 * d, grids)} for d in range(1, grids // 2)]
    barrier = pltpu.get_barrier_semaphore()
    for peer in peers:
        pl.semaphore_signal(barrier, inc=1, device_id=peer, device_id_type=pl.DeviceIdType.MESH)
    pl.semaphore_wait(barrier, len(peers))

    def remote(source, target, number):
        return pltpu.make_async_remote_copy(
            src_ref=source,
            dst_ref=target,
            send_sem=send_sems.at[number],
            recv_sem=recv_sems.at[number],
            device_id=peers[number],
            device_id_type=pl.DeviceIdType.MESH,
        )

    last, initial = pl.ds(slab - halo, halo), pl.ds(0, 1)
    sends = []
    for i, (source, target, peer) in enumerate(
        (
            (kap.at[0, last], kprev, up),
            (dens.at[0, last], dprev, up),
            (kap.at[0, initial], knext, down),
            (dens.at[0, initial], dnext, down),
        )
    ):
        copy = pltpu.make_async_remote_copy(
            src_ref=source,
            dst_ref=target,
            send_sem=halo_send.at[i],
            recv_sem=halo_recv.at[i],
            device_id=peer,
            device_id_type=pl.DeviceIdType.MESH,
        )
        copy.start()
        sends.append(copy)

    def natural(ref, row):
        return jnp.stack([ref[row, pl.ds(j, 8, stride=groups), :] for j in range(groups)], axis=0)

    def first(r, k_above, d_above, carry):
        k, d, flux = carry
        x_face = 0.5 * (k + k_above)
        y_face = 0.5 * (k + next_y(k))
        z_face = 0.5 * (k + next_lane(k))
        fx[r - 1] = x_face
        fy[r - 1] = y_face
        fz[r - 1] = z_face
        f_a[r - 1], flux = row_update(d, d_above, flux, x_face, y_face, z_face)
        return k_above, d_above, flux

    def both(x, carry):
        return first(x + halo, natural(raw_k, x), natural(raw_d, x), carry)

    zero = jnp.zeros((groups, 8, LANES), jnp.float32)
    for c in range(chunks):
        for copy in copies[c]:
            copy.wait()
        start, rest = c * chunk, chunk
        if c == 0:
            carry = (natural(raw_k, 0), natural(raw_d, 0), zero)
            start, rest = 1, chunk - 1

        def several(i, carry, start=start):
            for u in range(UNROLL):
                carry = both(start + i * UNROLL + u, carry)
            return carry

        carry = lax.fori_loop(0, rest // UNROLL, several, carry)
        for x in range(start + rest // UNROLL * UNROLL, start + rest):
            carry = both(x, carry)
    for copy in sends:
        copy.wait_recv()
    first(slab + halo, natural(knext, 0), natural(dnext, 0), carry)
    carry = (natural(kprev, 0), natural(dprev, 0), zero)
    for r in range(1, halo):
        carry = first(r, natural(kprev, r), natural(dprev, r), carry)
    carry = both(0, carry)
    f_a[halo] = f_a[halo] - carry[2]

    stride = plan.stride
    left = ITERS - 2
    old, new_f = f_a, f_b
    while 2 * left + 1 >= stride:
        low, high = halo - left, halo + slab - stride + left
        count, rest = (high - low + 1) // UNROLL, (high - low + 1) % UNROLL

        def one(r, carry, old=old, new_f=new_f):
            row, flux = carry
            above = old[r + 1]
            new_f[r], flux = row_update(row, above, flux, fx[r], fy[r], fz[r])
            return above, flux

        def several_steps(i, carry, low=low, one=one):
            for u in range(UNROLL):
                carry = one(low + UNROLL * i + u, carry)
            return carry

        row = old[low]
        flux = fx[low - 1] * (row - old[low - 1])
        carry = lax.fori_loop(0, count, several_steps, (row, flux))
        for r in range(low + UNROLL * count, high + 1):
            carry = one(r, carry)
        old, new_f = new_f, old
        left -= 1

    def cone_step(center, wanted, reach, old, new_f):
        def near(j, far):
            return any(min((j - w) % groups, (w - j) % groups) <= far for w in wanted)

        flux = {}
        for offset in range(-reach, reach + 1):
            need = [j for j in range(groups) if near(j, reach - abs(offset))]
            r = center + offset
            cells = {}

            def cell(j):
                if j not in cells:
                    cells[j] = old[r, j]
                return cells[j]

            below, flux, fluxes_y = flux, {}, {}

            def flux_y(j):
                if j not in fluxes_y:
                    follow = cell(j + 1) if j + 1 < groups else pltpu.roll(cell(0), 7, 0)
                    fluxes_y[j] = fy[r, j] * (follow - cell(j))
                return fluxes_y[j]

            for j in need:
                here = cell(j)
                flux[j] = fx[r, j] * (old[r + 1, j] - here)
                lower = below[j] if j in below else fx[r - 1, j] * (here - old[r - 1, j])
                before = flux_y(j - 1) if j else pltpu.roll(flux_y(groups - 1), 1, 0)
                gz = fz[r, j] * (next_lane(here) - here)
                new_f[r, j] = ((here + flux[j]) + (flux_y(j) + gz)) - ((lower + before) + last_lane(gz))

    period = min(8, plan.rows)

    def cones(i, _):
        source, target = old, new_f
        for reach in range(left, -1, -1):
            for k in range(period):
                spare = EXTRA if k == 0 else min(EXTRA, trailing_zeros(k))
                step = max(1, groups >> spare)
                center = halo + (i * period + k) * stride
                cone_step(center, list(range(0, groups, step)), reach, source, target)
            source, target = target, source
        return 0

    done = old if left % 2 else new_f

    def transform(k_low, k_high):
        part = [done[halo + k * stride].reshape(groups * 8, LANES) for k in range(k_low, k_high)]
        part = split_dot(jnp.concatenate(part, axis=0), hz[...], False)
        size, count = groups * 8, k_high - k_low
        part = jnp.concatenate([part[i * size : (i + 1) * size] for i in range(count)], axis=1)
        part = split_dot(hy[...], part, True)
        for i in range(count):
            planes[k_low + i] = part[:, i * LANES : (i + 1) * LANES]

    cones(0, 0)
    transform(0, 1)
    gathers = [remote(planes.at[0], coarse.at[here], i) for i in range(plan.members - 1)]
    for copy in gathers:
        copy.start()
    lax.fori_loop(1, plan.rows // period, cones, 0)
    transform(1, plan.rows)
    combine(plan, grids, here, remote, gathers, levels, coefs, ly, lz, planes, out, coarse, mine, pair, parts)
    for copy in sends:
        copy.wait_send()


def expand_kernel(plan, slab, pos_ref, levels, ly, lz, dy, dz, packed, out, coarse, nodes, buf, sems):
    mask = grid_mask(levels, ly, lz)
    members, rows, stride = plan.members, plan.rows, plan.stride
    where = {(row, q): (tile, lane) for row, q, tile, lane in plan.pieces}

    def total(row):
        parts = []
        for q in range(plan.blocks):
            if (row, q) in where:
                tile, lane = where[row, q]
                piece = packed[tile]
                if lane:
                    piece = pltpu.roll(piece, LANES - lane, 1)
                keep = mask[8 * q : 8 * q + 8] & (plan.levels[row] <= levels[0, 0])
                parts.append(jnp.where(keep, piece, 0.0))
            else:
                parts.append(jnp.zeros((8, LANES), jnp.float32))
        return jnp.concatenate(parts, axis=0)

    values = [total(p) for p in range(members)]
    h = members // 2
    while h:
        for p in range(h, members, 2 * h):
            values[p] = values[p] + 0.5 * (values[p - h] + values[(p + h) % members])
        h //= 2
    for p in range(members):
        coarse[p] = values[p]
    pos = pos_ref[0]
    fine = [coarse[pos]] + [total(members + k - 1) for k in range(1, rows)] + [coarse[lax.rem(pos + 1, members)]]
    h = rows // 2
    while h:
        for k in range(h, rows, 2 * h):
            fine[k] = fine[k] + 0.5 * (fine[k - h] + fine[k + h])
        h //= 2

    def chunk(k):
        part = pl.ds(k * stride, stride)
        return pltpu.make_async_copy(buf.at[part], out.at[0, part], sems.at[k])

    def fill(k, _):
        here = nodes[k]
        step = (nodes[k + 1] - here) * (1.0 / stride)
        for j in range(stride):
            buf[k * stride + j] = here + float(j) * step if j else here
        chunk(k).start()
        return 0

    def transform(low, high):
        size = fine[0].shape[0]
        part = split_dot(jnp.concatenate(fine[low:high], axis=0), dz[...], False)
        part = jnp.concatenate([part[i * size : (i + 1) * size] for i in range(high - low)], axis=1)
        part = split_dot(dy[...], part, True)
        for i in range(high - low):
            nodes[low + i] = part[:, i * LANES : (i + 1) * LANES]

    half = rows // 2
    transform(0, half + 1)
    lax.fori_loop(0, half, fill, 0)
    transform(half + 1, rows + 1)
    lax.fori_loop(half, rows, fill, 0)

    def drain(k, _):
        chunk(k).wait()
        return 0

    lax.fori_loop(0, rows, drain, 0)


def local(plan, density, kappa, levels, coefs):
    _, slab, width_y, width_z = density.shape
    groups = width_y // 8
    members = lax.axis_size("space")
    position = lax.axis_index("space")
    hy, hz, dy, dz, ly, lz = axis_tables(width_y, width_z)
    pos = jnp.reshape(position, (1,)).astype(jnp.int32)
    vmem = pl.BlockSpec(memory_space=pltpu.VMEM)
    smem = pl.BlockSpec(memory_space=pltpu.SMEM)
    anywhere = pl.BlockSpec(memory_space=pl.ANY)
    params = pltpu.CompilerParams(vmem_limit_bytes=VMEM_LIMIT)
    kept = ly.shape[0]
    chunk = min(32, slab)
    extended = pltpu.VMEM((slab + ITERS, groups, 8, LANES), jnp.float32)
    raw = pltpu.VMEM((slab, width_y, width_z), jnp.float32)
    below = pltpu.VMEM((ITERS, width_y, width_z), jnp.float32)
    above = pltpu.VMEM((1, width_y, width_z), jnp.float32)
    grids = lax.axis_size("grid")
    peers = members - 1 + grids // 2
    packed_shape = (plan.tiles, 8, LANES)
    packed = pl.pallas_call(
        functools.partial(surplus_kernel, plan, grids, slab, groups, chunk),
        out_shape=jax.ShapeDtypeStruct(packed_shape, jnp.float32),
        in_specs=[smem, smem, vmem, vmem, anywhere, anywhere, vmem, vmem],
        out_specs=vmem,
        scratch_shapes=[raw, raw, below, below, above, above]
        + [extended] * 5
        + [
            pltpu.VMEM((plan.rows, kept, LANES), jnp.float32),
            pltpu.VMEM((members, kept, LANES), jnp.float32),
            pltpu.VMEM(packed_shape, jnp.float32),
            pltpu.VMEM(packed_shape, jnp.float32),
            pltpu.VMEM((grids // 2,) + packed_shape, jnp.float32),
            pltpu.SemaphoreType.DMA((2, slab // chunk)),
            pltpu.SemaphoreType.DMA((4,)),
            pltpu.SemaphoreType.DMA((4,)),
            pltpu.SemaphoreType.DMA((peers,)),
            pltpu.SemaphoreType.DMA((peers,)),
        ],
        compiler_params=pltpu.CompilerParams(vmem_limit_bytes=VMEM_LIMIT, collective_id=0, has_side_effects=True),
        name="surplus",
    )(levels, coefs, ly, lz, density, kappa, hy, hz)

    return pl.pallas_call(
        functools.partial(expand_kernel, plan, slab),
        out_shape=jax.ShapeDtypeStruct(density.shape, jnp.float32),
        in_specs=[smem, smem] + [vmem] * 5,
        out_specs=anywhere,
        scratch_shapes=[
            pltpu.VMEM((plan.members, kept, LANES), jnp.float32),
            pltpu.VMEM((plan.rows + 1, width_y, width_z), jnp.float32),
            raw,
            pltpu.SemaphoreType.DMA((plan.rows,)),
        ],
        compiler_params=params,
        name="expand",
    )(pos, levels, ly, lz, dy, dz, packed)


def solution(mesh):
    def whole(density, kappa, levels, coefs):
        members = mesh.shape["space"]
        plan = Plan(members, density.shape[1] // members, density.shape[2], density.shape[3])
        in_specs = (
            P("grid", "space", None, None),
            P("grid", "space", None, None),
            P("grid", None),
            P("grid"),
        )
        out_specs = P("grid", "space", None, None)
        body = functools.partial(local, plan)
        return jax.shard_map(body, mesh=mesh, in_specs=in_specs, out_specs=out_specs, check_vma=False)(density, kappa, levels, coefs)

    return whole
```
